512 devices in a mesh: dp: 16 (over y, z_lo), factor: 32 (over z_hi, x, core).
Axes of the slice: x: 4, y: 4, z: 16 (z_hi: 4, z_lo: 4; z = z_hi * 4 + z_lo), core: 2. Of those that a mesh axis runs over, the one named last changes fastest.
Arguments:
- acts: bfloat16 [2048, 6144], P('dp', 'factor'), may hold values from -6 to 6
- grads_out: bfloat16 [2048, 12288], P('dp', 'factor'), may hold values from -6 to 6
- owners: int32 [136], replicated, may hold values from 0 to 31, as said below
Outputs:
- panel_rows: float32 [32, 6, 128, 512], P('factor', None, 'dp')
- precond_block: float32 [512, 512], P('factor')
The draws below stay inside these ranges and needn't reach their ends.
Inputs may be any that keep to these rules, and one draw needn't show every extreme that they name: `owners`: each owner holds at most 6 tiles, and one owner holds exactly 6 in every draw.
All inputs are finite; a program needn't handle non-finite values.
Results may differ from the reference program's by a relative error of at most 0.0003.
Values may be sent and summed in bfloat16 or wider, within the bound.
A program may use at most 64 MiB of HBM per device.

```python
import jax
import jax.numpy as jnp

D = 6144
FW = 12288
PANEL = 512
TILE = 128
TOKENS = 2048
NT = 136
CAP = 6
N_FACTOR = 32


def draw_owners(key, part):
    key = jax.random.fold_in(key, 11)
    key_heavy, key_order, key_shift = jax.random.split(key, 3)
    heavy = jax.random.randint(key_heavy, (), 0, N_FACTOR)
    order = jax.random.permutation(key_order, NT)
    shift = jax.random.randint(key_shift, (), 0, N_FACTOR - 1)
    position = jnp.arange(NT, dtype=jnp.int32)
    others = (position - CAP + shift) % (N_FACTOR - 1)
    others = others + (others >= heavy).astype(jnp.int32)
    owner_at = jnp.where(position < CAP, heavy, others).astype(jnp.int32)
    return jnp.zeros((NT,), jnp.int32).at[order].set(owner_at)


def block_levels(stream_key, dims, shards, least, high):
    def one(dim, shards_of):
        heights = jax.random.uniform(jax.random.fold_in(jax.random.fold_in(stream_key, 6), dim), (shards_of,), jnp.float32, least / len(shards), high / len(shards))
        return jnp.repeat(jnp.exp(heights), dims[dim] // shards_of).reshape((-1,) + (1,) * (len(dims) - dim - 1))

    level = one(*shards[0])
    for cut in shards[1:]:
        level = level * one(*cut)
    return level


def centred(rng, shape, scale, limit, shards=(), kind=jnp.bfloat16):
    gain = block_levels(rng, shape, shards, -0.22, 0.18) if shards else 1.0
    values = jax.random.normal(rng, shape, jnp.float32) * scale * gain
    return jnp.minimum(jnp.maximum(values, -limit), limit).astype(kind)


def setup_inputs(seed: int = 0) -> dict:
    arg_keys = jax.random.split(jax.random.key(seed), 4)
    acts = centred(arg_keys[0], (TOKENS, D), 1.0, 6.0, ((0, 16), (1, 32)))
    grads_out = centred(arg_keys[1], (TOKENS, FW), 1.0, 6.0, ((0, 16), (1, 32)))
    owners = draw_owners(jax.random.fold_in(arg_keys[3], 71), 0)
    return dict(acts=acts, grads_out=grads_out, owners=owners)


damping = 0.1

def reference(acts, grads_out, owners):
    tokens = acts.shape[0]
    a_panel = jnp.dot(acts.T.astype(jnp.float32), acts[:, :PANEL].astype(jnp.float32), preferred_element_type=jnp.float32) / tokens
    g_panel = jnp.dot(grads_out.T.astype(jnp.float32), grads_out[:, :PANEL].astype(jnp.float32), preferred_element_type=jnp.float32) / tokens
    grad_block = jnp.dot(grads_out[:, :PANEL].T.astype(jnp.float32), acts[:, :PANEL].astype(jnp.float32), preferred_element_type=jnp.float32) / tokens
    eye = jnp.eye(PANEL, dtype=jnp.float32)
    chol_a = jnp.linalg.cholesky(a_panel[:PANEL] + damping * eye)
    chol_g = jnp.linalg.cholesky(g_panel[:PANEL] + damping * eye)
    rest_a = jax.scipy.linalg.solve_triangular(chol_a, a_panel[PANEL:].T, lower=True).T
    rest_g = jax.scipy.linalg.solve_triangular(chol_g, g_panel[PANEL:].T, lower=True).T
    tiles = jnp.concatenate([rest_a, rest_g], axis=0).reshape(NT, TILE, PANEL)
    owner_ids = jnp.arange(N_FACTOR, dtype=jnp.int32)
    match = (owners[None, :] == owner_ids[:, None]).astype(jnp.int32)
    rank = jnp.cumsum(match, axis=1).astype(jnp.int32) - 1
    slot_ids = jnp.arange(CAP, dtype=jnp.int32)
    select = (match[:, None, :] == 1) & (rank[:, None, :] == slot_ids[None, :, None])
    valid = jnp.any(select, axis=2)
    tile_ids = jnp.sum(select.astype(jnp.int32) * jnp.arange(NT, dtype=jnp.int32)[None, None, :], axis=2).astype(jnp.int32)
    panel_rows = jnp.where(valid[:, :, None, None], tiles[tile_ids], jnp.float32(0.0))
    half = jax.scipy.linalg.solve_triangular(chol_g, grad_block, lower=True)
    precond_block = jax.scipy.linalg.solve_triangular(chol_a, half.T, lower=True).T
    return (panel_rows, precond_block)
```

```python
import jax
import jax.numpy as jnp
from jax import lax
from jax.experimental import pallas as pl
from jax.experimental.pallas import tpu as pltpu
from jax.sharding import PartitionSpec as P

D = 6144
PANEL = 512
TILE = 128
NT = 136
TILES_A = (D - PANEL) // TILE
CAP = 6
BLK = 128
GROUPS = 5
FROWS = 48

damping = 0.1
MESH = pl.DeviceIdType.MESH
HIGH = lax.Precision.HIGHEST


def lanes(x, c):
    return jnp.broadcast_to(x[:, :, c:c + 1], x.shape)


def rows8(x, j):
    return jnp.broadcast_to(x[:, j:j + 1, :], x.shape)


def strip16(x0, x1, w0, w1, c0, sub):
    b0 = [lanes(x0, c0 + j) for j in range(16)]
    b1 = [lanes(x1, c0 + j) for j in range(16)]
    d0 = jnp.ones(x0.shape, jnp.float32)
    d1 = d0
    for j in range(8):
        piv = rows8(b0[j], j)
        d0 = jnp.where(sub == j, piv, d0)
        inv = 1.0 / piv
        m0 = jnp.where(sub > j, b0[j] * inv, 0.0)
        m1 = b1[j] * inv
        for k in range(j + 1, 16):
            r = rows8(b0[k], j)
            b0[k] = b0[k] - m0 * r
            b1[k] = b1[k] - m1 * r
        r = rows8(x0, j)
        x0 = x0 - m0 * r
        x1 = x1 - m1 * r
        r = rows8(w0, j)
        w0 = w0 - m0 * r
        w1 = w1 - m1 * r
    for j in range(8):
        piv = rows8(b1[8 + j], j)
        d1 = jnp.where(sub == j, piv, d1)
        if j == 7:
            break
        m1 = jnp.where(sub > j, b1[8 + j] * (1.0 / piv), 0.0)
        for k in range(j + 1, 8):
            b1[8 + k] = b1[8 + k] - m1 * rows8(b1[8 + k], j)
        x1 = x1 - m1 * rows8(x1, j)
        w1 = w1 - m1 * rows8(w1, j)
    s0, s1 = lax.rsqrt(d0), lax.rsqrt(d1)
    s0 = s0 * (1.5 - 0.5 * d0 * s0 * s0)
    s1 = s1 * (1.5 - 0.5 * d1 * s1 * s1)
    return x0 * s0, x1 * s1, w0 * s0, w1 * s1


def factor_blocks(x, out):
    sub = lax.broadcasted_iota(jnp.int32, (2, 8, BLK), 1)
    w = jnp.where(lax.broadcasted_iota(jnp.int32, (2, BLK, BLK), 1)
                  == lax.broadcasted_iota(jnp.int32, (2, BLK, BLK), 2), 1.0, 0.0).astype(jnp.float32)
    for i in range(8):
        v0, v1, u0, u1 = strip16(x[:, 0:8], x[:, 8:16], w[:, 0:8], w[:, 8:16], 16 * i, sub)
        out[:, 16 * i:16 * i + 8, :] = u0
        out[:, 16 * i + 8:16 * i + 16, :] = u1
        if i == 7:
            break
        x, w = x[:, 16:], w[:, 16:]
        lo = 16 * (i + 1)
        for v, u in ((v0, u0), (v1, u1)):
            vt = jnp.stack([v[0].T, v[1].T])[:, lo:, :]
            for j in range(8):
                m = jnp.broadcast_to(vt[:, :, j:j + 1], x.shape)
                x = x - m * v[:, j:j + 1, :]
                w = w - m * u[:, j:j + 1, :]


def dot32(a, b, dims):
    return lax.dot_general(a, b, (dims, ((), ())), precision=HIGH, preferred_element_type=jnp.float32)


def dot16(a, b, dims):
    return lax.dot_general(a, b, (dims, ((), ())), preferred_element_type=jnp.float32)


def owned_table(own_ref, d, f):
    def look(t, carry):
        n, slots = carry[0], carry[1:]
        hit = own_ref[t] == f
        slots = tuple(
            jnp.where(jnp.logical_and(hit, n == s), t, slots[s]) for s in range(CAP))
        return (n + hit.astype(jnp.int32),) + slots

    zero = jnp.int32(0)
    found = lax.fori_loop(0, NT, look, (zero,) + (zero,) * CAP)
    n, p = found[0], lax.div(d, 8)
    table = []
    for s in range(CAP):
        t = found[1 + s]
        half = 2 * (t + 4) + p
        fa = lax.div(half, 3)
        slot_a = lax.div(half - 3 * fa - lax.rem(3 * fa + p, 2), 2)
        tg = jnp.maximum(t - TILES_A, 0) + 4
        fg = lax.div(tg, 3)
        slot_g = 2 + tg - 3 * fg
        is_act = (t < TILES_A).astype(jnp.int32)
        place = jnp.where(is_act == 1, fa * GROUPS + slot_a, fg * GROUPS + slot_g)
        table.append((place, is_act, (s < n).astype(jnp.int32)))
    return table


def kernel(own_ref, za, gr, fs, rows_out, pre_out,
           pan, feat, z0, z1, mat, inv, inv0, wmat, raw, allr, picked,
           s_one, r_one, s_z, r_blk, s_y, s_half, r_half, s_sib, r_sib, s_f, r_f,
           s_gz, s_gx, s_gs, r_g):
    d = lax.axis_index("dp")
    f = lax.axis_index("factor")
    y, zl = lax.div(d, 4), lax.rem(d, 4)
    role, zh, core = lax.rem(f, 8), lax.div(f, 8), lax.rem(f, 2)
    xx = lax.div(role, 2)
    base = f - role
    sib = f + 1 - 2 * core
    scale = 1.0 / 2048.0

    def z_peer(k):
        return lax.rem(f + 8 * k, 32)

    def x_peer(k):
        return base + 2 * lax.rem(xx + k, 4) + core

    def copy(src, dst, send, recv, to):
        return pltpu.make_async_remote_copy(
            src_ref=src, dst_ref=dst, send_sem=send, recv_sem=recv,
            device_id=to, device_id_type=MESH)

    barrier = pltpu.get_barrier_semaphore()
    for k in range(1, 16):
        pl.semaphore_signal(barrier, inc=1, device_id=(lax.rem(d + k, 16), f), device_id_type=MESH)
    for k in range(1, 4):
        pl.semaphore_signal(barrier, inc=1, device_id=(d, z_peer(k)), device_id_type=MESH)
        pl.semaphore_signal(barrier, inc=1, device_id=(d, x_peer(k)), device_id_type=MESH)
    pl.semaphore_signal(barrier, inc=1, device_id=(d, sib), device_id_type=MESH)
    pl.semaphore_wait(barrier, 22)

    places = [
        (0, z0),
        (0, pan.at[1, d, :, pl.ds(0, 384)]),
        (1, z1),
        (1, pan.at[1, d, :, pl.ds(384, 128)]),
        (2, pan.at[0, d, :, pl.ds(384, 128)]),
    ]
    held = [[n for n in range(5) if places[n][0] == r] for r in range(3)]

    def piece(n, slot, to):
        return copy(places[n][1], places[n][1], s_one.at[n, slot], r_one.at[n], (d, to))

    @pl.when(f == 0)
    def _():
        z0[...] = za[...]
        pan[1, d, :, 0:384] = gr[...]

    @pl.when(f == 1)
    def _():
        z1[...] = za[...]
        pan[1, d, :, 384:512] = gr[:, 0:128]

    @pl.when(f == 2)
    def _():
        pan[0, d, :, 384:512] = za[:, 0:128]

    for r in range(3):
        @pl.when(f == r)
        def _():
            for k in (1, 3, 2):
                for n in held[r]:
                    piece(n, k - 1, z_peer(k)).start()

        @pl.when(jnp.logical_and(role == r, zh > 0))
        def _():
            for n in held[r]:
                piece(n, 0, sib).wait_recv()

        @pl.when(role == r)
        def _():
            for k in (1, 3, 2):
                for n in held[r]:
                    piece(n, 2 + k, x_peer(k)).start()
            for n in held[r]:
                piece(n, 6, sib).start()

    def features(k):
        to = lax.rem(d + k, 16)
        return copy(fs.at[to], feat.at[d], s_f.at[k], r_f.at[k], (to, f))

    for k in range(1, 16):
        features(k).start()
    feat[d] = fs[d]
    mat[...] = jnp.zeros_like(mat)
    wmat[...] = jnp.zeros_like(wmat)
    raw[...] = jnp.zeros_like(raw)
    inv[...] = jnp.zeros_like(inv)

    for r in range(3):
        @pl.when(jnp.logical_and(core == r % 2, role != r))
        def _():
            for n in held[r]:
                piece(n, 0, sib).wait_recv()
                piece(n, 6, sib).start()
    for r in range(3):
        @pl.when(core != r % 2)
        def _():
            for n in held[r]:
                piece(n, 0, sib).wait_recv()

    pan[0, d, :, 0:128] = z0[:, 0:128]
    pan[0, d, :, 128:256] = z0[:, 128:256] + z1[:, 0:128]
    pan[0, d, :, 256:384] = z1[:, 128:256]

    def at(dy, dz):
        return lax.rem(y + 4 - dy, 4) * 4 + lax.rem(zl + 4 - dz, 4)

    def y_dev(dy):
        return (lax.rem(y + dy, 4) * 4 + zl, f)

    def block(which, sem, to):
        return copy(pan.at[core, which], pan.at[core, which], sem, r_blk.at[which], to)

    def z_copy(dz):
        return block(d, s_z.at[dz], (y * 4 + lax.rem(zl + dz, 4), f))

    def y_copy(dz, way):
        return block(at(0, dz), s_y.at[dz, way], y_dev((1, 3)[way]))

    def half_copy(dz, way):
        which = at((1, 3)[way], dz)
        ref = pan.at[core, which, pl.ds(64 * way, 64)]
        return copy(ref, ref, s_half.at[dz, way], r_half.at[way, which], y_dev((1, 3)[way]))

    def half_in(dz, way):
        which = at(2, dz)
        ref = pan.at[core, which, pl.ds(64 * way, 64)]
        return copy(ref, ref, s_half.at[dz, way], r_half.at[way, which], y_dev(1))

    def sibling(dy, dz):
        which = at(dy, dz)
        return copy(pan.at[core, which], pan.at[core, which], s_sib.at[dy * 4 + dz], r_sib.at[which], (d, sib))

    def from_sibling(dy, dz):
        which = at(dy, dz)
        return copy(pan.at[1 - core, which], pan.at[1 - core, which], s_sib.at[1], r_sib.at[which], (d, sib))

    order = (0, 1, 3, 2)
    for dz in (1, 3, 2):
        z_copy(dz).start()
    for way in range(2):
        y_copy(0, way).start()
    for dz in (1, 3, 2):
        block(at(0, dz), s_z.at[dz], y_dev(1)).wait_recv()
        for way in range(2):
            y_copy(dz, way).start()
        sibling(0, dz).start()

    def line(dy):
        return pl.ds(pl.multiple_of(lax.rem(y + 4 - dy, 4) * 4, 4), 4)

    def ready(dy):
        for dz in range(4):
            if dy or dz:
                from_sibling(dy, dz).wait_recv()

    def sum_a(dy):
        pa = pan[0, line(dy)].reshape(512, PANEL)
        mat[0] = mat[0] + dot16(pa, pa, ((0,), (0,)))

    def sum_g(dy):
        pg = pan[1, line(dy)].reshape(512, PANEL)
        mat[1] = mat[1] + dot16(pg, pg, ((0,), (0,)))

    def sum_w(dy):
        pa = pan[0, line(dy)].reshape(512, PANEL)
        pg = pan[1, line(dy)].reshape(512, PANEL)
        wmat[...] = wmat[...] + dot16(pg, pa, ((0,), (0,)))

    def sum_rows(dy):
        ra = jnp.zeros((16, PANEL), jnp.float32)
        rg = jnp.zeros((32, PANEL), jnp.float32)
        for dz in range(4):
            which = at(dy, dz)
            ra = ra + dot16(feat[which, 0:16, :], pan[0, which], ((1,), (0,)))
            rg = rg + dot16(feat[which, 16:48, :], pan[1, which], ((1,), (0,)))
        raw[0:16, :] = raw[0:16, :] + ra
        raw[16:48, :] = raw[16:48, :] + rg

    work = (sum_a, sum_g, sum_w, sum_rows)
    ready(0)
    for k in range(1, 16):
        src = lax.rem(d + 16 - k, 16)
        copy(fs.at[d], feat.at[src], s_f.at[k], r_f.at[k], (lax.rem(d + 1, 16), f)).wait_recv()
    for step in range(4):
        dz = order[step]
        for way in range(2):
            block(at((1, 3)[way], dz), s_z.at[1], y_dev(1)).wait_recv()
            half_copy(dz, way).start()
            sibling((1, 3)[way], dz).start()
        work[step](0)
    ready(1)
    for step in range(4):
        dz = order[step]
        for way in range(2):
            half_in(dz, way).wait_recv()
        sibling(2, dz).start()
        work[step](1)
    ready(3)
    for fn in work:
        fn(3)
    ready(2)
    sum_rows(2)

    for s in range(GROUPS):
        allr[f, s] = raw[8 * s:8 * s + 8, :] * scale

    def g_z(k):
        return copy(allr.at[f], allr.at[f], s_gz.at[k], r_g.at[f], (d, z_peer(k)))

    def g_x(q, k):
        src = lax.rem(f + 8 * q, 32)
        return copy(allr.at[src], allr.at[src], s_gx.at[q, k], r_g.at[src], (d, x_peer(k)))

    def g_from(q, k):
        return lax.rem(zh + q, 4) * 8 + 2 * lax.rem(xx + k, 4) + core

    def g_sib(q, k):
        src = g_from(q, k)
        return copy(allr.at[src], allr.at[src], s_gs.at[q, k], r_g.at[src], (d, sib))

    def g_in(src):
        return copy(allr.at[src], allr.at[src], s_gz.at[0], r_g.at[src], (d, sib))

    for k in (1, 3, 2):
        g_z(k).start()
        g_x(0, k).start()
    g_sib(0, 0).start()

    sum_a(2)
    sum_g(2)
    sum_w(2)

    r_i = lax.broadcasted_iota(jnp.int32, (PANEL, PANEL), 0)
    c_i = lax.broadcasted_iota(jnp.int32, (PANEL, PANEL), 1)
    shift = jnp.where(r_i == c_i, jnp.float32(damping), jnp.float32(0.0))
    mat[0] = mat[0] * scale + shift
    mat[1] = mat[1] * scale + shift

    def step(k, carry):
        start = pl.multiple_of(k * BLK, BLK)
        factor_blocks(mat[:, pl.ds(start, BLK), pl.ds(start, BLK)], inv0)
        for kk in range(4):
            @pl.when(k == kk)
            def _():
                lo, hi = kk * BLK, (kk + 1) * BLK
                for n in range(2):
                    li = inv0[n]
                    inv[n, lo:hi, lo:hi] = li
                    if kk > 0:
                        inv[n, lo:hi, 0:lo] = dot32(li, inv[n, lo:hi, 0:lo], ((1,), (0,)))
                    if kk < 3:
                        u = dot32(li, mat[n, lo:hi, hi:PANEL], ((1,), (0,)))
                        mat[n, hi:PANEL, hi:PANEL] = mat[n, hi:PANEL, hi:PANEL] - dot32(u, u, ((0,), (0,)))
                        inv[n, hi:PANEL, 0:hi] = inv[n, hi:PANEL, 0:hi] - dot32(
                            u, inv[n, lo:hi, 0:hi], ((0,), (0,)))
                if kk == 1:
                    for q in (1, 3, 2):
                        g_in(g_from(q, 0)).wait_recv()
                        for k2 in (1, 3, 2):
                            g_x(q, k2).start()
                        g_sib(q, 0).start()
        return carry

    lax.fori_loop(0, 4, step, 0)
    for q in range(4):
        for k in (1, 3, 2):
            g_in(g_from(q, k)).wait_recv()
            g_sib(q, k).start()

    mine = pl.multiple_of(f * 16, 16)
    half = dot32(inv[1, pl.ds(mine, 16), :], wmat[...] * scale, ((1,), (0,)))
    pre_out[...] = dot32(half, inv[0], ((1,), (1,)))

    table = owned_table(own_ref, d, f)
    for q in range(4):
        for k in range(4):
            g_in(g_from(q, k) + 1 - 2 * core).wait_recv()
    for s in range(CAP):
        picked[8 * s:8 * s + 8, :] = allr[lax.div(table[s][0], GROUPS), lax.rem(table[s][0], GROUPS)]
    rows = picked[...]
    ra, rg = dot32(rows, inv[0], ((1,), (1,))), dot32(rows, inv[1], ((1,), (1,)))
    for s in range(CAP):
        lo, hi = 8 * s, 8 * s + 8
        out = jnp.where(jnp.full((8, PANEL), table[s][1]) == 1, ra[lo:hi, :], rg[lo:hi, :])
        rows_out[s] = jnp.where(jnp.full((8, PANEL), table[s][2]) == 1, out, 0.0)

    for r in range(3):
        @pl.when(f == r)
        def _():
            for k in (1, 2, 3):
                for n in held[r]:
                    piece(n, k - 1, z_peer(k)).wait_send()

        @pl.when(role == r)
        def _():
            for k in (1, 2, 3):
                for n in held[r]:
                    piece(n, 2 + k, x_peer(k)).wait_send()

        @pl.when(core == r % 2)
        def _():
            for n in held[r]:
                piece(n, 6, sib).wait_send()

    for k in range(1, 16):
        features(k).wait_send()
        sibling(k // 4, k % 4).wait_send()
    for k in (1, 2, 3):
        z_copy(k).wait_send()
        g_z(k).wait_send()
    for dz in range(4):
        for way in range(2):
            y_copy(dz, way).wait_send()
            half_copy(dz, way).wait_send()
        for k in (1, 2, 3):
            g_x(dz, k).wait_send()
        for k in range(4):
            g_sib(dz, k).wait_send()


def window(owners, za, gr, fs):
    vmem = pl.BlockSpec(memory_space=pltpu.VMEM)
    dma = pltpu.SemaphoreType.DMA
    f32, bf16 = jnp.float32, jnp.bfloat16
    return pl.pallas_call(
        kernel,
        out_shape=(
            jax.ShapeDtypeStruct((CAP, 8, PANEL), f32),
            jax.ShapeDtypeStruct((16, PANEL), f32),
        ),
        in_specs=[pl.BlockSpec(memory_space=pltpu.SMEM)] + [vmem] * 3,
        out_specs=(vmem, vmem),
        scratch_shapes=[
            pltpu.VMEM((2, 16, 128, PANEL), bf16),
            pltpu.VMEM((16, FROWS, 128), bf16),
            pltpu.VMEM((128, 256), bf16),
            pltpu.VMEM((128, 256), bf16),
            pltpu.VMEM((2, PANEL, PANEL), f32),
            pltpu.VMEM((2, PANEL, PANEL), f32),
            pltpu.VMEM((2, BLK, BLK), f32),
            pltpu.VMEM((PANEL, PANEL), f32),
            pltpu.VMEM((FROWS, PANEL), f32),
            pltpu.VMEM((32, GROUPS, 8, PANEL), f32),
            pltpu.VMEM((8 * CAP, PANEL), f32),
            dma((5, 7)), dma((5,)),
            dma((4,)), dma((16,)), dma((4, 2)),
            dma((4, 2)), dma((2, 16)),
            dma((16,)), dma((16,)),
            dma((16,)), dma((16,)),
            dma((4,)), dma((4, 4)), dma((4, 4)), dma((32,)),
        ],
        compiler_params=pltpu.CompilerParams(
            collective_id=0, has_side_effects=True, vmem_limit_bytes=48 * 2**20),
        name="window",
    )(owners, za, gr, fs)


def feature_slots(acts, grads_out, odd):
    x = acts.T.reshape(3, 8, 8, 128)
    both = jnp.stack([x[0], x[2]])
    one = jnp.stack([x[1], x[1]])
    first = jnp.where(odd, one, both)
    second = jnp.where(odd, both, one)
    a = jnp.stack([first, second]).transpose(0, 2, 1, 3, 4).reshape(16, 16, 128)
    g = grads_out.T.reshape(3, 16, 8, 128).transpose(1, 0, 2, 3).reshape(16, 24, 128)
    return jnp.concatenate([a, g, jnp.zeros((16, 8, 128), a.dtype)], axis=1)


def on_device(acts, grads_out, owners):
    odd = lax.rem(lax.axis_index("factor"), 2) == 1
    zero = jnp.zeros((128, 64), acts.dtype)
    za = jnp.where(odd, jnp.concatenate([zero, acts], 1), jnp.concatenate([acts, zero], 1))
    rows, pre = window(owners, za, grads_out, feature_slots(acts, grads_out, odd))
    return rows[None], pre


def solution(mesh):
    return jax.shard_map(
        on_device,
        mesh=mesh,
        in_specs=(P("dp", "factor"), P("dp", "factor"), P()),
        out_specs=(P("factor", None, "dp", None), P("factor", None)),
        check_vma=False,
    )
```

```python
import jax
import jax.numpy as jnp
from jax import lax
from jax.experimental import pallas as pl
from jax.experimental.pallas import tpu as pltpu
from jax.sharding import PartitionSpec as P

D = 6144
PANEL = 512
TILE = 128
NT = 136
TILES_A = (D - PANEL) // TILE
CAP = 6
BLK = 128
GROUPS = 5
FROWS = 48

damping = 0.1
MESH = pl.DeviceIdType.MESH
HIGH = lax.Precision.HIGHEST


def lanes(x, c):
    return jnp.broadcast_to(x[:, :, c:c + 1], x.shape)


def rows8(x, j):
    return jnp.broadcast_to(x[:, j:j + 1, :], x.shape)


def recip(x):
    r = pl.reciprocal(x, approx=True)
    r = r * (2.0 - x * r)
    return r * (2.0 - x * r)


def pair(ba, bb, j):
    p00, p01, p11 = rows8(ba, j), rows8(bb, j), rows8(bb, j + 1)
    det = p00 * p11 - p01 * p01
    r0, rd = recip(p00), recip(det)
    return p00, p01, det, r0, rd


def strip16(x0, x1, w0, w1, c0, sub):
    b0 = [lanes(x0, c0 + j) for j in range(16)]
    b1 = [lanes(x1, c0 + j) for j in range(16)]
    d0 = jnp.ones(x0.shape, jnp.float32)
    d1 = d0
    for j in range(0, 8, 2):
        ba, bb = b0[j], b0[j + 1]
        p00, p01, det, r0, rd = pair(ba, bb, j)
        d0 = jnp.where(sub == j, p00, jnp.where(sub == j + 1, det * r0, d0))
        q = p01 * r0
        m0a = jnp.where(sub > j, ba, 0.0) * r0
        m0b = jnp.where(sub > j + 1, bb * p00 - ba * p01, 0.0) * rd
        m1a = b1[j] * r0
        m1b = (b1[j + 1] * p00 - b1[j] * p01) * rd
        for k in range(j + 2, 16):
            ra = rows8(b0[k], j)
            rb = rows8(b0[k], j + 1) - q * ra
            b0[k] = b0[k] - m0a * ra - m0b * rb
            b1[k] = b1[k] - m1a * ra - m1b * rb
        ra = rows8(x0, j)
        rb = rows8(x0, j + 1) - q * ra
        x0 = x0 - m0a * ra - m0b * rb
        x1 = x1 - m1a * ra - m1b * rb
        ra = rows8(w0, j)
        rb = rows8(w0, j + 1) - q * ra
        w0 = w0 - m0a * ra - m0b * rb
        w1 = w1 - m1a * ra - m1b * rb
    for j in range(0, 8, 2):
        ba, bb = b1[8 + j], b1[9 + j]
        p00, p01, det, r0, rd = pair(ba, bb, j)
        d1 = jnp.where(sub == j, p00, jnp.where(sub == j + 1, det * r0, d1))
        q = p01 * r0
        ma = jnp.where(sub > j, ba, 0.0) * r0
        mb = jnp.where(sub > j + 1, bb * p00 - ba * p01, 0.0) * rd
        for k in range(j + 2, 8):
            ra = rows8(b1[8 + k], j)
            rb = rows8(b1[8 + k], j + 1) - q * ra
            b1[8 + k] = b1[8 + k] - ma * ra - mb * rb
        ra = rows8(x1, j)
        rb = rows8(x1, j + 1) - q * ra
        x1 = x1 - ma * ra - mb * rb
        ra = rows8(w1, j)
        rb = rows8(w1, j + 1) - q * ra
        w1 = w1 - ma * ra - mb * rb
    s0, s1 = lax.rsqrt(d0), lax.rsqrt(d1)
    s0 = s0 * (1.5 - 0.5 * d0 * s0 * s0)
    s1 = s1 * (1.5 - 0.5 * d1 * s1 * s1)
    return x0 * s0, x1 * s1, w0 * s0, w1 * s1


def factor_blocks(x, out):
    sub = lax.broadcasted_iota(jnp.int32, (2, 8, BLK), 1)
    w = jnp.where(lax.broadcasted_iota(jnp.int32, (2, BLK, BLK), 1)
                  == lax.broadcasted_iota(jnp.int32, (2, BLK, BLK), 2), 1.0, 0.0).astype(jnp.float32)
    for i in range(8):
        v0, v1, u0, u1 = strip16(x[:, 0:8], x[:, 8:16], w[:, 0:8], w[:, 8:16], 16 * i, sub)
        out[:, 16 * i:16 * i + 8, :] = u0
        out[:, 16 * i + 8:16 * i + 16, :] = u1
        if i == 7:
            break
        x, w = x[:, 16:], w[:, 16:]
        lo = 16 * (i + 1)
        for v, u in ((v0, u0), (v1, u1)):
            vt = jnp.stack([v[0].T, v[1].T])[:, lo:, :]
            for j in range(8):
                m = jnp.broadcast_to(vt[:, :, j:j + 1], x.shape)
                x = x - m * v[:, j:j + 1, :]
                w = w - m * u[:, j:j + 1, :]


def dot32(a, b, dims):
    return lax.dot_general(a, b, (dims, ((), ())), precision=HIGH, preferred_element_type=jnp.float32)


def dot16(a, b, dims):
    return lax.dot_general(a, b, (dims, ((), ())), preferred_element_type=jnp.float32)


def owned_tables(own_ref, d, ids):
    zero = jnp.int32(0)

    def look(t, carry):
        owner = own_ref[t]
        out = []
        for n, *slots in carry:
            hit = owner == ids[len(out)]
            slots = [jnp.where(jnp.logical_and(hit, n == s), t, slots[s]) for s in range(CAP)]
            out.append((n + hit.astype(jnp.int32),) + tuple(slots))
        return tuple(out)

    found = lax.fori_loop(0, NT, look, tuple((zero,) * (CAP + 1) for _ in ids))
    p = lax.div(d, 8)
    tables = []
    for n, *slots in found:
        table = []
        for s in range(CAP):
            t = slots[s]
            half = 2 * (t + 4) + p
            fa = lax.div(half, 3)
            slot_a = lax.div(half - 3 * fa - lax.rem(3 * fa + p, 2), 2)
            tg = jnp.maximum(t - TILES_A, 0) + 4
            fg = lax.div(tg, 3)
            slot_g = 2 + tg - 3 * fg
            act = t < TILES_A
            table.append((
                jnp.where(act, fa, fg), jnp.where(act, slot_a, slot_g),
                act.astype(jnp.int32), (s < n).astype(jnp.int32)))
        tables.append(table)
    return tables


def kernel(own_in, at_in, gr_in, rows_out, pre_out,
           own_ref, act_t, gr, fs, za, pan, feat, z1, mat, inv0, invt, wmat, raw, loc, pack, got, picked,
           s_in, s_p, r_p, s_b, s_c, r_own, s_z, r_blk, s_y, s_far, r_far, s_x, r_x, s_sib, r_sib, s_f, r_f,
           s_lx, s_ls, r_l, s_g, r_g):
    d = lax.axis_index("dp")
    f = lax.axis_index("factor")
    y, zl = lax.div(d, 4), lax.rem(d, 4)
    role, zh, core = lax.rem(f, 8), lax.div(f, 8), lax.rem(f, 2)
    xx = lax.div(role, 2)
    base = f - role
    sib = f + 1 - 2 * core
    scale = 1.0 / 2048.0

    def z_peer(k):
        return lax.rem(f + 8 * k, 32)

    def x_peer(k):
        return base + 2 * lax.rem(xx + k, 4) + core

    def copy(src, dst, send, recv, to):
        return pltpu.make_async_remote_copy(
            src_ref=src, dst_ref=dst, send_sem=send, recv_sem=recv,
            device_id=to, device_id_type=MESH)

    fetch = (
        pltpu.make_async_copy(at_in, act_t, s_in.at[0]),
        pltpu.make_async_copy(gr_in, gr, s_in.at[1]),
        pltpu.make_async_copy(own_in, own_ref, s_in.at[2]),
    )
    for c in fetch:
        c.start()

    barrier = pltpu.get_barrier_semaphore()
    for k in range(1, 16):
        pl.semaphore_signal(barrier, inc=1, device_id=(lax.rem(d + k, 16), f), device_id_type=MESH)
    for k in range(1, 4):
        pl.semaphore_signal(barrier, inc=1, device_id=(d, z_peer(k)), device_id_type=MESH)
        pl.semaphore_signal(barrier, inc=1, device_id=(d, x_peer(k)), device_id_type=MESH)
    pl.semaphore_signal(barrier, inc=1, device_id=(d, sib), device_id_type=MESH)
    for c in fetch:
        c.wait()

    odd = core == 1

    @pl.when(f < 3)
    def _():
        at32 = act_t[...].astype(jnp.float32)
        gap = jnp.zeros((64, 128), jnp.float32)
        placed = jnp.where(odd, jnp.concatenate([gap, at32], 0), jnp.concatenate([at32, gap], 0))
        za[...] = placed.T.astype(jnp.bfloat16)

    pl.semaphore_wait(barrier, 22)

    h = lax.rem(xx, 2)

    def half_of(parity):
        return pl.ds(pl.multiple_of(64 * parity, 64), 64)

    def part(way):
        return pl.ds(pl.multiple_of(64 * h + 32 * way, 32), 32)

    def other_part(way):
        return pl.ds(pl.multiple_of(64 * (1 - h) + 32 * way, 32), 32)

    give_g = copy(gr, pan.at[1, d, :, pl.ds(0, 384)], s_p.at[0], r_p.at[2], (d, f + 1))
    give_z1 = copy(za, z1, s_p.at[0], r_p.at[0], (d, lax.rem(f + 31, 32)))
    give_t3 = copy(za.at[:, pl.ds(0, 128)], pan.at[0, d, :, pl.ds(384, 128)], s_p.at[0], r_p.at[1],
                   (d, lax.rem(f + 30, 32)))

    def own_x(k):
        rows = pl.ds(64 * (k % 2), 64)
        return copy(pan.at[core, d, rows], pan.at[core, d, rows], s_b.at[k], r_own, (d, x_peer(k)))

    def own_z(k):
        ref = pan.at[core, d, half_of(h)]
        return copy(ref, ref, s_c.at[k], r_own, (d, z_peer(k)))

    @pl.when(f == 0)
    def _():
        give_g.start()
        copy(za, z1, s_p.at[0], r_p.at[0], (d, f + 1)).wait_recv()
        pan[0, d, :, 0:128] = za[:, 0:128]
        pan[0, d, :, 128:256] = za[:, 128:256] + z1[:, 0:128]
        pan[0, d, :, 256:384] = z1[:, 128:256]
        copy(za.at[:, pl.ds(0, 128)], pan.at[0, d, :, pl.ds(384, 128)], s_p.at[0], r_p.at[1], (d, f + 1)).wait_recv()

    @pl.when(f == 1)
    def _():
        give_z1.start()
        pan[1, d, :, 384:512] = gr[:, 0:128]
        copy(gr, pan.at[1, d, :, pl.ds(0, 384)], s_p.at[0], r_p.at[2], (d, f + 1)).wait_recv()

    @pl.when(f == 2)
    def _():
        give_t3.start()

    @pl.when(f < 2)
    def _():
        for k in (1, 3, 2):
            own_x(k).start()

    @pl.when(jnp.logical_and(zh == 0, xx > 0))
    def _():
        own_z(1).wait_recv()

    @pl.when(zh == 0)
    def _():
        for k in (1, 3, 2):
            own_z(k).start()

    at32 = act_t[...].astype(jnp.float32)
    gt32 = gr[...].astype(jnp.float32).T
    for t in range(16):
        p, q = t // 8, t % 8
        low = at32[8 * q:8 * q + 8]
        mid = at32[64 + 8 * q:72 + 8 * q]
        top = at32[128 + 8 * q:136 + 8 * q]
        here = odd if p else jnp.logical_not(odd)
        fs[t, 0:16, :] = jnp.concatenate(
            [jnp.where(here, low, mid), jnp.where(here, top, mid)], 0).astype(jnp.bfloat16)
        gs = [gt32[128 * i + 8 * t:128 * i + 8 * t + 8] for i in range(3)]
        fs[t, 16:48, :] = jnp.concatenate(gs + [jnp.zeros_like(gs[0])], 0).astype(jnp.bfloat16)

    def features(k):
        to = lax.rem(d + k, 16)
        return copy(fs.at[to], feat.at[d], s_f.at[k], r_f.at[k], (to, f))

    for k in range(1, 16):
        features(k).start()
    feat[d] = fs[d]
    mat[...] = jnp.zeros_like(mat)
    invt[...] = jnp.zeros_like(invt)
    wmat[...] = jnp.zeros_like(wmat)
    raw[...] = jnp.zeros_like(raw)
    tables = owned_tables(own_ref, d, [f] + [z_peer(k) for k in range(1, 4)])

    @pl.when(zh > 0)
    def _():
        own_z(1).wait_recv()

    def at(dy, dz):
        return lax.rem(y + 4 - dy, 4) * 4 + lax.rem(zl + 4 - dz, 4)

    def y_dev(dy):
        return (lax.rem(y + dy, 4) * 4 + zl, f)

    def block(which, sem, to):
        ref = pan.at[core, which, half_of(h)]
        return copy(ref, ref, sem, r_blk.at[which], to)

    def z_copy(dz):
        return block(d, s_z.at[dz], (y * 4 + lax.rem(zl + dz, 4), f))

    def y_copy(dz, way):
        return block(at(0, dz), s_y.at[dz, way], y_dev((1, 3)[way]))

    def far_copy(dz, way):
        which = at((1, 3)[way], dz)
        ref = pan.at[core, which, part(way)]
        return copy(ref, ref, s_far.at[dz, way], r_far.at[way, which], y_dev((1, 3)[way]))

    def far_in(dz, way):
        which = at(2, dz)
        ref = pan.at[core, which, part(way)]
        return copy(ref, ref, s_far.at[dz, way], r_far.at[way, which], y_dev(1))

    def x_copy(dy, dz, way):
        which = at(dy, dz)
        ref = pan.at[core, which, part(way)]
        return copy(ref, ref, s_x.at[way, dy * 4 + dz], r_x.at[way, which], (d, x_peer((1, 3)[way])))

    def x_in(dy, dz, way):
        which = at(dy, dz)
        ref = pan.at[core, which, other_part(way)]
        return copy(ref, ref, s_x.at[way, 0], r_x.at[way, which], (d, x_peer(1)))

    holder = jnp.logical_and(zh == 0, xx == 0)

    def own_to_x(way, act):
        to_holder = jnp.logical_and(zh == 0, xx == (3, 1)[way])

        @pl.when(jnp.logical_not(to_holder))
        def _():
            act(x_copy(0, 0, way))

    def sibling(dy, dz):
        which = at(dy, dz)
        return copy(pan.at[core, which], pan.at[core, which], s_sib.at[dy * 4 + dz], r_sib.at[which], (d, sib))

    def whole(dy, dz):
        if dy or dz:
            for way in range(2):
                x_in(dy, dz, way).wait_recv()
        else:
            @pl.when(jnp.logical_not(holder))
            def _():
                for way in range(2):
                    x_in(dy, dz, way).wait_recv()
        sibling(dy, dz).start()

    def from_sibling(dy, dz):
        which = at(dy, dz)
        return copy(pan.at[1 - core, which], pan.at[1 - core, which], s_sib.at[1], r_sib.at[which], (d, sib))

    for dz in (1, 3, 2):
        z_copy(dz).start()
    for way in range(2):
        y_copy(0, way).start()
    for way in range(2):
        own_to_x(way, lambda c: c.start())
    for dz in (1, 3, 2):
        block(at(0, dz), s_z.at[dz], y_dev(1)).wait_recv()
        for way in range(2):
            y_copy(dz, way).start()
        for way in range(2):
            x_copy(0, dz, way).start()

    def line(dy):
        return pl.ds(pl.multiple_of(lax.rem(y + 4 - dy, 4) * 4, 4), 4)

    def ready(dy):
        for dz in range(4):
            from_sibling(dy, dz).wait_recv()

    def add_upper(n, cols, cols_t):
        mat[n, 0:256, 0:PANEL] = mat[n, 0:256, 0:PANEL] + dot16(cols_t[0:256], cols, ((1,), (0,)))
        mat[n, 256:PANEL, 256:PANEL] = mat[n, 256:PANEL, 256:PANEL] + dot16(
            cols_t[256:PANEL], cols[:, 256:PANEL], ((1,), (0,)))

    def sum_a(dy):
        pa = pan[0, line(dy)].reshape(512, PANEL)
        add_upper(0, pa, pa.T)

    def sum_g(dy):
        pg = pan[1, line(dy)].reshape(512, PANEL)
        add_upper(1, pg, pg.T)

    def sum_w(dy):
        pa = pan[0, line(dy)].reshape(512, PANEL)
        pg = pan[1, line(dy)].reshape(512, PANEL)
        wmat[...] = wmat[...] + dot16(pg.T, pa, ((1,), (0,)))

    def sum_rows(dy):
        ra = jnp.zeros((16, PANEL), jnp.float32)
        rg = jnp.zeros((32, PANEL), jnp.float32)
        for dz in range(4):
            which = at(dy, dz)
            ra = ra + dot16(feat[which, 0:16, :], pan[0, which], ((1,), (0,)))
            rg = rg + dot16(feat[which, 16:48, :], pan[1, which], ((1,), (0,)))
        raw[0:16, :] = raw[0:16, :] + ra
        raw[16:48, :] = raw[16:48, :] + rg

    def near(dz):
        for way in range(2):
            block(at((1, 3)[way], dz), s_z.at[1], y_dev(1)).wait_recv()
            far_copy(dz, way).start()
            for to in range(2):
                x_copy((1, 3)[way], dz, to).start()

    def far(dz):
        for way in range(2):
            far_in(dz, way).wait_recv()
            x_copy(2, dz, way).start()

    for dz in (0, 1, 3, 2):
        near(dz)
        whole(0, dz)
    far(0)
    ready(0)
    sum_a(0)
    far(1)
    for dz in (0, 1, 3, 2):
        whole(1, dz)
    sum_g(0)
    far(3)
    for dz in (0, 1, 3, 2):
        whole(3, dz)
    ready(1)
    sum_a(1)
    far(2)
    for k in range(1, 16):
        src = lax.rem(d + 16 - k, 16)
        copy(fs.at[d], feat.at[src], s_f.at[k], r_f.at[k], (lax.rem(d + 1, 16), f)).wait_recv()
    sum_rows(0)
    sum_g(1)
    for dz in (0, 1, 3, 2):
        whole(2, dz)
    sum_rows(1)
    ready(3)
    sum_a(3)
    sum_rows(3)
    ready(2)
    sum_rows(2)

    for s in range(GROUPS):
        loc[role, s] = raw[8 * s:8 * s + 8, :] * scale

    def l_x(k):
        return copy(loc.at[role], loc.at[role], s_lx.at[k], r_l.at[role], (d, x_peer(k)))

    def l_role(k):
        return 2 * lax.rem(xx + k, 4) + core

    def l_sib(k):
        r = l_role(k)
        return copy(loc.at[r], loc.at[r], s_ls.at[k], r_l.at[r], (d, sib))

    def l_in(r):
        return copy(loc.at[r], loc.at[r], s_ls.at[0], r_l.at[r], (d, sib))

    def slots(k):
        return copy(pack.at[k], got.at[zh], s_g.at[k], r_g.at[zh], (d, z_peer(k)))

    for k in (1, 3, 2):
        l_x(k).start()
    l_sib(0).start()

    sum_g(3)
    for k in (1, 3, 2):
        l_in(l_role(k)).wait_recv()
        l_sib(k).start()
    sum_a(2)
    sum_g(2)
    for k in range(4):
        l_in(l_role(k) + 1 - 2 * core).wait_recv()
    for k in (1, 3, 2):
        for s in range(CAP):
            place = tables[k][s]
            pack[k, s] = loc[lax.rem(place[0], 8), place[1]]
        slots(k).start()
    for s in range(CAP):
        place = tables[0][s]
        got[zh, s] = loc[lax.rem(place[0], 8), place[1]]

    eye = jnp.where(lax.broadcasted_iota(jnp.int32, (BLK, BLK), 0) == lax.broadcasted_iota(jnp.int32, (BLK, BLK), 1),
                    jnp.float32(damping), jnp.float32(0.0))

    def block_at(n, i, j, width=BLK):
        b = mat[n, i * BLK:(i + 1) * BLK, j * BLK:j * BLK + width] * scale
        if i == j:
            diag = b[:, 0:BLK] + eye
            b = diag if width == BLK else jnp.concatenate([diag, b[:, BLK:]], 1)
        return b

    for n in range(2):
        for i in range(4):
            mat[n, i * BLK:(i + 1) * BLK, i * BLK:PANEL] = block_at(n, i, i, PANEL - i * BLK)

    x = mat[:, 0:BLK, 0:BLK]
    for kk in range(4):
        lo, hi = kk * BLK, (kk + 1) * BLK
        factor_blocks(x, inv0.at[kk])
        sum_w(kk)
        li = [inv0[kk, n] for n in range(2)]
        if kk < 3:
            first = [dot32(li[n], mat[n, lo:hi, hi:hi + BLK], ((1,), (0,))) for n in range(2)]
            first_t = [v.T for v in first]
            x = jnp.stack([
                mat[n, hi:hi + BLK, hi:hi + BLK] - dot32(first_t[n], first[n], ((1,), (0,))) for n in range(2)])
        for n in range(2):
            mat[n, lo:hi, PANEL + lo:PANEL + hi] = li[n]
            if kk < 3:
                rest = PANEL + lo - hi - BLK
                if rest:
                    mat[n, lo:hi, hi + BLK:PANEL + lo] = dot32(li[n], mat[n, lo:hi, hi + BLK:PANEL + lo], ((1,), (0,)))
                row = mat[n, lo:hi, hi + BLK:PANEL + hi]
                mat[n, hi:hi + BLK, hi + BLK:PANEL + hi] = mat[n, hi:hi + BLK, hi + BLK:PANEL + hi] - dot32(
                    first_t[n], row, ((1,), (0,)))
                for i in range(kk + 2, 4):
                    ut = mat[n, lo:hi, i * BLK:(i + 1) * BLK].T
                    mat[n, i * BLK:(i + 1) * BLK, i * BLK:PANEL + hi] = mat[
                        n, i * BLK:(i + 1) * BLK, i * BLK:PANEL + hi] - dot32(
                        ut, mat[n, lo:hi, i * BLK:PANEL + hi], ((1,), (0,)))
            elif kk == 3:
                mat[n, lo:hi, PANEL:PANEL + lo] = dot32(li[n], mat[n, lo:hi, PANEL:PANEL + lo], ((1,), (0,)))
            invt[n, 0:hi, lo:hi] = mat[n, lo:hi, PANEL:PANEL + hi].T

    mine = pl.multiple_of(f * 16, 16)
    picked[8 * CAP:, :] = dot32(mat[1, pl.ds(mine, 16), PANEL:] * scale, wmat[...], ((1,), (0,)))
    for k in range(1, 4):
        src = lax.rem(zh + k, 4)
        copy(pack.at[k], got.at[src], s_g.at[k], r_g.at[src], (d, z_peer(k))).wait_recv()
    table = tables[0]
    for s in range(CAP):
        picked[8 * s:8 * s + 8, :] = got[lax.div(table[s][0], 8), s]
    def times_inverse(n, rows):
        left = dot32(rows[:, 0:256], invt[n, 0:256, 0:256], ((1,), (0,)))
        return jnp.concatenate([left, dot32(rows, invt[n, :, 256:PANEL], ((1,), (0,)))], 1)

    ra = times_inverse(0, picked[...])
    rg = times_inverse(1, picked[0:8 * CAP, :])
    pre_out[...] = ra[8 * CAP:, :]
    for s in range(CAP):
        lo, hi = 8 * s, 8 * s + 8
        out = jnp.where(jnp.full((8, PANEL), table[s][2]) == 1, ra[lo:hi, :], rg[lo:hi, :])
        rows_out[s] = jnp.where(jnp.full((8, PANEL), table[s][3]) == 1, out, 0.0)

    @pl.when(f == 0)
    def _():
        give_g.wait_send()

    @pl.when(f == 1)
    def _():
        give_z1.wait_send()

    @pl.when(f == 2)
    def _():
        give_t3.wait_send()

    @pl.when(f < 2)
    def _():
        for k in (1, 2, 3):
            own_x(k).wait_send()

    @pl.when(zh == 0)
    def _():
        for k in (1, 2, 3):
            own_z(k).wait_send()

    for way in range(2):
        own_to_x(way, lambda c: c.wait_send())
    for k in range(1, 16):
        features(k).wait_send()
        for way in range(2):
            x_copy(k // 4, k % 4, way).wait_send()
    for k in range(16):
        sibling(k // 4, k % 4).wait_send()
    for k in (1, 2, 3):
        z_copy(k).wait_send()
        l_x(k).wait_send()
        slots(k).wait_send()
    for dz in range(4):
        for way in range(2):
            y_copy(dz, way).wait_send()
            far_copy(dz, way).wait_send()
        l_sib(dz).wait_send()


def window(owners, acts_t, grads_out):
    vmem = pl.BlockSpec(memory_space=pltpu.VMEM)
    dma = pltpu.SemaphoreType.DMA
    f32, bf16 = jnp.float32, jnp.bfloat16
    return pl.pallas_call(
        kernel,
        out_shape=(
            jax.ShapeDtypeStruct((CAP, 8, PANEL), f32),
            jax.ShapeDtypeStruct((16, PANEL), f32),
        ),
        in_specs=[pl.BlockSpec(memory_space=pltpu.HBM)] * 3,
        out_specs=(vmem, vmem),
        scratch_shapes=[
            pltpu.SMEM((NT,), jnp.int32),
            pltpu.VMEM((192, 128), bf16),
            pltpu.VMEM((128, 384), bf16),
            pltpu.VMEM((16, FROWS, 128), bf16),
            pltpu.VMEM((128, 256), bf16),
            pltpu.VMEM((2, 16, 128, PANEL), bf16),
            pltpu.VMEM((16, FROWS, 128), bf16),
            pltpu.VMEM((128, 256), bf16),
            pltpu.VMEM((2, PANEL, 2 * PANEL), f32),
            pltpu.VMEM((4, 2, BLK, BLK), f32),
            pltpu.VMEM((2, PANEL, PANEL), f32),
            pltpu.VMEM((PANEL, PANEL), f32),
            pltpu.VMEM((FROWS, PANEL), f32),
            pltpu.VMEM((8, GROUPS, 8, PANEL), f32),
            pltpu.VMEM((4, CAP, 8, PANEL), f32),
            pltpu.VMEM((4, CAP, 8, PANEL), f32),
            pltpu.VMEM((8 * CAP + 16, PANEL), f32),
            dma((3,)),
            dma((1,)), dma((3,)), dma((4,)), dma((4,)), dma,
            dma((4,)), dma((16,)), dma((4, 2)),
            dma((4, 2)), dma((2, 16)),
            dma((2, 16)), dma((2, 16)),
            dma((16,)), dma((16,)),
            dma((16,)), dma((16,)),
            dma((4,)), dma((4,)), dma((8,)),
            dma((4,)), dma((4,)),
        ],
        compiler_params=pltpu.CompilerParams(
            collective_id=0, has_side_effects=True, vmem_limit_bytes=60 * 2**20),
        name="window",
    )(owners, acts_t, grads_out)


def hand_over_kernel(rows, pre, rows_out, pre_out, sems):
    copies = (pltpu.make_async_copy(rows, rows_out, sems.at[0]), pltpu.make_async_copy(pre, pre_out, sems.at[1]))
    for c in copies:
        c.start()
    for c in copies:
        c.wait()


def hand_over(rows, pre):
    anywhere = pl.BlockSpec(memory_space=pl.ANY)
    return pl.pallas_call(
        hand_over_kernel,
        out_shape=(
            jax.ShapeDtypeStruct(rows.shape, rows.dtype),
            jax.ShapeDtypeStruct(pre.shape, pre.dtype),
        ),
        in_specs=[anywhere] * 2,
        out_specs=(anywhere, anywhere),
        scratch_shapes=[pltpu.SemaphoreType.DMA((2,))],
        compiler_params=pltpu.CompilerParams(vmem_limit_bytes=60 * 2**20),
        name="hand_over",
    )(rows, pre)


def on_device(acts, grads_out, owners):
    rows, pre = hand_over(*window(owners, acts.T, grads_out))
    return rows[None], pre


def solution(mesh):
    return jax.shard_map(
        on_device,
        mesh=mesh,
        in_specs=(P("dp", "factor"), P("dp", "factor"), P()),
        out_specs=(P("factor", None, "dp", None), P("factor", None)),
        check_vma=False,
    )
```

```python
import jax
import jax.numpy as jnp
from jax import lax
from jax.experimental import pallas as pl
from jax.experimental.pallas import tpu as pltpu
from jax.sharding import PartitionSpec as P

D = 6144
PANEL = 512
TILE = 128
NT = 136
TILES_A = (D - PANEL) // TILE
CAP = 6
BLK = 128
GROUPS = 5
FROWS = 48

damping = 0.1
MESH = pl.DeviceIdType.MESH
HIGH = lax.Precision.HIGHEST


def lanes(x, c):
    return jnp.broadcast_to(x[:, :, c:c + 1], x.shape)


def rows8(x, j):
    return jnp.broadcast_to(x[:, j:j + 1, :], x.shape)


def recip(x):
    r = pl.reciprocal(x, approx=True)
    r = r * (2.0 - x * r)
    return r * (2.0 - x * r)


def pair(ba, bb, j):
    p00, p01, p11 = rows8(ba, j), rows8(bb, j), rows8(bb, j + 1)
    det = p00 * p11 - p01 * p01
    r0, rd = recip(p00), recip(det)
    return p00, p01, det, r0, rd


def strip16(x0, x1, w0, w1, c0, sub):
    b0 = [lanes(x0, c0 + j) for j in range(16)]
    b1 = [lanes(x1, c0 + j) for j in range(16)]
    d0 = jnp.ones(x0.shape, jnp.float32)
    d1 = d0
    for j in range(0, 8, 2):
        ba, bb = b0[j], b0[j + 1]
        p00, p01, det, r0, rd = pair(ba, bb, j)
        d0 = jnp.where(sub == j, p00, jnp.where(sub == j + 1, det * r0, d0))
        q = p01 * r0
        m0a = jnp.where(sub > j, ba, 0.0) * r0
        m0b = jnp.where(sub > j + 1, bb * p00 - ba * p01, 0.0) * rd
        m1a = b1[j] * r0
        m1b = (b1[j + 1] * p00 - b1[j] * p01) * rd
        for k in range(j + 2, 16):
            ra = rows8(b0[k], j)
            rb = rows8(b0[k], j + 1) - q * ra
            b0[k] = b0[k] - m0a * ra - m0b * rb
            b1[k] = b1[k] - m1a * ra - m1b * rb
        ra = rows8(x0, j)
        rb = rows8(x0, j + 1) - q * ra
        x0 = x0 - m0a * ra - m0b * rb
        x1 = x1 - m1a * ra - m1b * rb
        ra = rows8(w0, j)
        rb = rows8(w0, j + 1) - q * ra
        w0 = w0 - m0a * ra - m0b * rb
        w1 = w1 - m1a * ra - m1b * rb
    for j in range(0, 8, 2):
        ba, bb = b1[8 + j], b1[9 + j]
        p00, p01, det, r0, rd = pair(ba, bb, j)
        d1 = jnp.where(sub == j, p00, jnp.where(sub == j + 1, det * r0, d1))
        q = p01 * r0
        ma = jnp.where(sub > j, ba, 0.0) * r0
        mb = jnp.where(sub > j + 1, bb * p00 - ba * p01, 0.0) * rd
        for k in range(j + 2, 8):
            ra = rows8(b1[8 + k], j)
            rb = rows8(b1[8 + k], j + 1) - q * ra
            b1[8 + k] = b1[8 + k] - ma * ra - mb * rb
        ra = rows8(x1, j)
        rb = rows8(x1, j + 1) - q * ra
        x1 = x1 - ma * ra - mb * rb
        ra = rows8(w1, j)
        rb = rows8(w1, j + 1) - q * ra
        w1 = w1 - ma * ra - mb * rb
    s0, s1 = lax.rsqrt(d0), lax.rsqrt(d1)
    s0 = s0 * (1.5 - 0.5 * d0 * s0 * s0)
    s1 = s1 * (1.5 - 0.5 * d1 * s1 * s1)
    return x0 * s0, x1 * s1, w0 * s0, w1 * s1


def factor_blocks(x, out):
    sub = lax.broadcasted_iota(jnp.int32, (2, 8, BLK), 1)
    w = jnp.where(lax.broadcasted_iota(jnp.int32, (2, BLK, BLK), 1)
                  == lax.broadcasted_iota(jnp.int32, (2, BLK, BLK), 2), 1.0, 0.0).astype(jnp.float32)
    for i in range(8):
        v0, v1, u0, u1 = strip16(x[:, 0:8], x[:, 8:16], w[:, 0:8], w[:, 8:16], 16 * i, sub)
        out[:, 16 * i:16 * i + 8, :] = u0
        out[:, 16 * i + 8:16 * i + 16, :] = u1
        if i == 7:
            break
        lo = 16 * (i + 1)
        v = jnp.concatenate([v0, v1], 1)
        u = jnp.concatenate([u0, u1], 1)
        vt = jnp.stack([v[0].T, v[1].T])
        nx, nw = x[:, 16:32], w[:, 16:32]
        for j in range(16):
            m = jnp.broadcast_to(vt[:, lo:lo + 16, j:j + 1], nx.shape)
            nx = nx - m * v[:, j:j + 1, :]
            nw = nw - m * u[:, j:j + 1, :]
        if i == 6:
            x, w = nx, nw
            continue
        vu = jnp.concatenate([v, u], 2)
        less = jnp.stack([dot32(vt[n, lo + 16:, :], vu[n], ((1,), (0,))) for n in range(2)])
        x = jnp.concatenate([nx, x[:, 32:] - less[:, :, 0:BLK]], 1)
        w = jnp.concatenate([nw, w[:, 32:] - less[:, :, BLK:]], 1)


def dot32(a, b, dims):
    return lax.dot_general(a, b, (dims, ((), ())), precision=HIGH, preferred_element_type=jnp.float32)


def dot16(a, b, dims):
    return lax.dot_general(a, b, (dims, ((), ())), preferred_element_type=jnp.float32)


def owned_tables(own_ref, d, ids):
    zero = jnp.int32(0)

    def look(t, carry):
        owner = own_ref[t]
        out = []
        for n, *slots in carry:
            hit = owner == ids[len(out)]
            slots = [jnp.where(jnp.logical_and(hit, n == s), t, slots[s]) for s in range(CAP)]
            out.append((n + hit.astype(jnp.int32),) + tuple(slots))
        return tuple(out)

    found = lax.fori_loop(0, NT, look, tuple((zero,) * (CAP + 1) for _ in ids))
    p = lax.div(d, 8)
    tables = []
    for n, *slots in found:
        table = []
        for s in range(CAP):
            t = slots[s]
            half = 2 * (t + 4) + p
            fa = lax.div(half, 3)
            slot_a = lax.div(half - 3 * fa - lax.rem(3 * fa + p, 2), 2)
            tg = jnp.maximum(t - TILES_A, 0) + 4
            fg = lax.div(tg, 3)
            slot_g = 2 + tg - 3 * fg
            act = t < TILES_A
            table.append((
                jnp.where(act, fa, fg), jnp.where(act, slot_a, slot_g),
                act.astype(jnp.int32), (s < n).astype(jnp.int32)))
        tables.append(table)
    return tables


def kernel(own_in, at_in, gr_in, rows_out, pre_out,
           own_ref, act_t, gr, fs, za, pan, feat, z1, mat, inv0, invt, wmat, raw, loc, pack, got, picked,
           s_in, s_p, r_p, s_b, s_c, r_own, s_z, r_blk, s_y, s_far, r_far, s_x, r_x, s_sib, r_sib, s_f, r_f,
           s_lx, s_ls, r_l, s_g, r_g):
    d = lax.axis_index("dp")
    f = lax.axis_index("factor")
    y, zl = lax.div(d, 4), lax.rem(d, 4)
    role, zh, core = lax.rem(f, 8), lax.div(f, 8), lax.rem(f, 2)
    xx = lax.div(role, 2)
    base = f - role
    sib = f + 1 - 2 * core
    scale = 1.0 / 2048.0

    def z_peer(k):
        return lax.rem(f + 8 * k, 32)

    def x_peer(k):
        return base + 2 * lax.rem(xx + k, 4) + core

    def copy(src, dst, send, recv, to):
        return pltpu.make_async_remote_copy(
            src_ref=src, dst_ref=dst, send_sem=send, recv_sem=recv,
            device_id=to, device_id_type=MESH)

    fetch = (
        pltpu.make_async_copy(at_in, act_t, s_in.at[0]),
        pltpu.make_async_copy(gr_in, gr, s_in.at[1]),
        pltpu.make_async_copy(own_in, own_ref, s_in.at[2]),
    )
    for c in fetch:
        c.start()

    barrier = pltpu.get_barrier_semaphore()
    for k in range(1, 16):
        pl.semaphore_signal(barrier, inc=1, device_id=(lax.rem(d + k, 16), f), device_id_type=MESH)
    for k in range(1, 4):
        pl.semaphore_signal(barrier, inc=1, device_id=(d, z_peer(k)), device_id_type=MESH)
        pl.semaphore_signal(barrier, inc=1, device_id=(d, x_peer(k)), device_id_type=MESH)
    pl.semaphore_signal(barrier, inc=1, device_id=(d, sib), device_id_type=MESH)
    for c in fetch:
        c.wait()

    odd = core == 1

    @pl.when(f < 3)
    def _():
        at32 = act_t[...].astype(jnp.float32)
        gap = jnp.zeros((64, 128), jnp.float32)
        placed = jnp.where(odd, jnp.concatenate([gap, at32], 0), jnp.concatenate([at32, gap], 0))
        za[...] = placed.T.astype(jnp.bfloat16)

    pl.semaphore_wait(barrier, 22)

    h = lax.rem(xx, 2)

    def half_of(parity):
        return pl.ds(pl.multiple_of(64 * parity, 64), 64)

    def part(way):
        return pl.ds(pl.multiple_of(64 * h + 32 * way, 32), 32)

    def other_part(way):
        return pl.ds(pl.multiple_of(64 * (1 - h) + 32 * way, 32), 32)

    give_g = copy(gr, pan.at[1, d, :, pl.ds(0, 384)], s_p.at[0], r_p.at[2], (d, f + 1))
    give_z1 = copy(za, z1, s_p.at[0], r_p.at[0], (d, lax.rem(f + 31, 32)))
    give_t3 = copy(za.at[:, pl.ds(0, 128)], pan.at[0, d, :, pl.ds(384, 128)], s_p.at[0], r_p.at[1],
                   (d, lax.rem(f + 30, 32)))

    def own_x(k):
        rows = pl.ds(64 * (k % 2), 64)
        return copy(pan.at[core, d, rows], pan.at[core, d, rows], s_b.at[k], r_own, (d, x_peer(k)))

    def own_z(k):
        ref = pan.at[core, d, half_of(h)]
        return copy(ref, ref, s_c.at[k], r_own, (d, z_peer(k)))

    @pl.when(f == 0)
    def _():
        give_g.start()
        copy(za, z1, s_p.at[0], r_p.at[0], (d, f + 1)).wait_recv()
        pan[0, d, :, 0:128] = za[:, 0:128]
        pan[0, d, :, 128:256] = za[:, 128:256] + z1[:, 0:128]
        pan[0, d, :, 256:384] = z1[:, 128:256]
        copy(za.at[:, pl.ds(0, 128)], pan.at[0, d, :, pl.ds(384, 128)], s_p.at[0], r_p.at[1], (d, f + 1)).wait_recv()

    @pl.when(f == 1)
    def _():
        give_z1.start()
        pan[1, d, :, 384:512] = gr[:, 0:128]
        copy(gr, pan.at[1, d, :, pl.ds(0, 384)], s_p.at[0], r_p.at[2], (d, f + 1)).wait_recv()

    @pl.when(f == 2)
    def _():
        give_t3.start()

    @pl.when(f < 2)
    def _():
        for k in (1, 3, 2):
            own_x(k).start()

    @pl.when(jnp.logical_and(zh == 0, xx > 0))
    def _():
        own_z(1).wait_recv()

    @pl.when(zh == 0)
    def _():
        for k in (1, 3, 2):
            own_z(k).start()

    at32 = act_t[...].astype(jnp.float32)
    gt32 = gr[...].astype(jnp.float32).T
    for t in range(16):
        p, q = t // 8, t % 8
        low = at32[8 * q:8 * q + 8]
        mid = at32[64 + 8 * q:72 + 8 * q]
        top = at32[128 + 8 * q:136 + 8 * q]
        here = odd if p else jnp.logical_not(odd)
        fs[t, 0:16, :] = jnp.concatenate(
            [jnp.where(here, low, mid), jnp.where(here, top, mid)], 0).astype(jnp.bfloat16)
        gs = [gt32[128 * i + 8 * t:128 * i + 8 * t + 8] for i in range(3)]
        fs[t, 16:48, :] = jnp.concatenate(gs + [jnp.zeros_like(gs[0])], 0).astype(jnp.bfloat16)

    def features(k):
        to = lax.rem(d + k, 16)
        return copy(fs.at[to], feat.at[d], s_f.at[k], r_f.at[k], (to, f))

    for k in range(1, 16):
        features(k).start()
    feat[d] = fs[d]
    mat[...] = jnp.zeros_like(mat)
    invt[...] = jnp.zeros_like(invt)
    wmat[...] = jnp.zeros_like(wmat)
    raw[...] = jnp.zeros_like(raw)
    tables = owned_tables(own_ref, d, [f] + [z_peer(k) for k in range(1, 4)])

    @pl.when(zh > 0)
    def _():
        own_z(1).wait_recv()

    def at(dy, dz):
        return lax.rem(y + 4 - dy, 4) * 4 + lax.rem(zl + 4 - dz, 4)

    def y_dev(dy):
        return (lax.rem(y + dy, 4) * 4 + zl, f)

    def block(which, sem, to):
        ref = pan.at[core, which, half_of(h)]
        return copy(ref, ref, sem, r_blk.at[which], to)

    def z_copy(dz):
        return block(d, s_z.at[dz], (y * 4 + lax.rem(zl + dz, 4), f))

    def y_copy(dz, way):
        return block(at(0, dz), s_y.at[dz, way], y_dev((1, 3)[way]))

    def far_copy(dz, way):
        which = at((1, 3)[way], dz)
        ref = pan.at[core, which, part(way)]
        return copy(ref, ref, s_far.at[dz, way], r_far.at[way, which], y_dev((1, 3)[way]))

    def far_in(dz, way):
        which = at(2, dz)
        ref = pan.at[core, which, part(way)]
        return copy(ref, ref, s_far.at[dz, way], r_far.at[way, which], y_dev(1))

    def x_copy(dy, dz, way):
        which = at(dy, dz)
        ref = pan.at[core, which, part(way)]
        return copy(ref, ref, s_x.at[way, dy * 4 + dz], r_x.at[way, which], (d, x_peer((1, 3)[way])))

    def x_in(dy, dz, way):
        which = at(dy, dz)
        ref = pan.at[core, which, other_part(way)]
        return copy(ref, ref, s_x.at[way, 0], r_x.at[way, which], (d, x_peer(1)))

    holder = jnp.logical_and(zh == 0, xx == 0)

    def own_to_x(way, act):
        to_holder = jnp.logical_and(zh == 0, xx == (3, 1)[way])

        @pl.when(jnp.logical_not(to_holder))
        def _():
            act(x_copy(0, 0, way))

    def sibling(dy, dz):
        which = at(dy, dz)
        return copy(pan.at[core, which], pan.at[core, which], s_sib.at[dy * 4 + dz], r_sib.at[which], (d, sib))

    def whole(dy, dz):
        if dy or dz:
            for way in range(2):
                x_in(dy, dz, way).wait_recv()
        else:
            @pl.when(jnp.logical_not(holder))
            def _():
                for way in range(2):
                    x_in(dy, dz, way).wait_recv()
        sibling(dy, dz).start()

    def from_sibling(dy, dz):
        which = at(dy, dz)
        return copy(pan.at[1 - core, which], pan.at[1 - core, which], s_sib.at[1], r_sib.at[which], (d, sib))

    for dz in (1, 3, 2):
        z_copy(dz).start()
    for way in range(2):
        y_copy(0, way).start()
    for way in range(2):
        own_to_x(way, lambda c: c.start())
    for dz in (1, 3, 2):
        block(at(0, dz), s_z.at[dz], y_dev(1)).wait_recv()
        for way in range(2):
            y_copy(dz, way).start()
        for way in range(2):
            x_copy(0, dz, way).start()

    def line(dy):
        return pl.ds(pl.multiple_of(lax.rem(y + 4 - dy, 4) * 4, 4), 4)

    def ready(dy):
        for dz in range(4):
            from_sibling(dy, dz).wait_recv()

    def add_upper(n, cols, cols_t):
        mat[n, 0:256, 0:PANEL] = mat[n, 0:256, 0:PANEL] + dot16(cols_t[0:256], cols, ((1,), (0,)))
        mat[n, 256:PANEL, 256:PANEL] = mat[n, 256:PANEL, 256:PANEL] + dot16(
            cols_t[256:PANEL], cols[:, 256:PANEL], ((1,), (0,)))

    def sum_a(dy):
        pa = pan[0, line(dy)].reshape(512, PANEL)
        add_upper(0, pa, pa.T)

    def sum_g(dy):
        pg = pan[1, line(dy)].reshape(512, PANEL)
        add_upper(1, pg, pg.T)

    def sum_w(dy):
        pa = pan[0, line(dy)].reshape(512, PANEL)
        pg = pan[1, line(dy)].reshape(512, PANEL)
        wmat[...] = wmat[...] + dot16(pg.T, pa, ((1,), (0,)))

    def sum_rows(dy):
        ra = jnp.zeros((16, PANEL), jnp.float32)
        rg = jnp.zeros((32, PANEL), jnp.float32)
        for dz in range(4):
            which = at(dy, dz)
            ra = ra + dot16(feat[which, 0:16, :], pan[0, which], ((1,), (0,)))
            rg = rg + dot16(feat[which, 16:48, :], pan[1, which], ((1,), (0,)))
        raw[0:16, :] = raw[0:16, :] + ra
        raw[16:48, :] = raw[16:48, :] + rg

    def near(dz):
        for way in range(2):
            block(at((1, 3)[way], dz), s_z.at[1], y_dev(1)).wait_recv()
            far_copy(dz, way).start()
            for to in range(2):
                x_copy((1, 3)[way], dz, to).start()

    def far(dz):
        for way in range(2):
            far_in(dz, way).wait_recv()
            x_copy(2, dz, way).start()

    for dz in (0, 1, 3, 2):
        near(dz)
        whole(0, dz)
    far(0)
    ready(0)
    sum_a(0)
    far(1)
    for dz in (0, 1, 3, 2):
        whole(1, dz)
    sum_g(0)
    far(3)
    for dz in (0, 1, 3, 2):
        whole(3, dz)
    ready(1)
    sum_a(1)
    far(2)
    for k in range(1, 16):
        src = lax.rem(d + 16 - k, 16)
        copy(fs.at[d], feat.at[src], s_f.at[k], r_f.at[k], (lax.rem(d + 1, 16), f)).wait_recv()
    sum_rows(0)
    sum_g(1)
    for dz in (0, 1, 3, 2):
        whole(2, dz)
    sum_rows(1)
    ready(3)
    sum_a(3)
    sum_rows(3)
    ready(2)
    sum_rows(2)

    for s in range(GROUPS):
        loc[role, s] = raw[8 * s:8 * s + 8, :] * scale

    def l_x(k):
        return copy(loc.at[role], loc.at[role], s_lx.at[k], r_l.at[role], (d, x_peer(k)))

    def l_role(k):
        return 2 * lax.rem(xx + k, 4) + core

    def l_sib(k):
        r = l_role(k)
        return copy(loc.at[r], loc.at[r], s_ls.at[k], r_l.at[r], (d, sib))

    def l_in(r):
        return copy(loc.at[r], loc.at[r], s_ls.at[0], r_l.at[r], (d, sib))

    def slots(k):
        return copy(pack.at[k], got.at[zh], s_g.at[k], r_g.at[zh], (d, z_peer(k)))

    for k in (1, 3, 2):
        l_x(k).start()
    l_sib(0).start()

    sum_g(3)
    for k in (1, 3, 2):
        l_in(l_role(k)).wait_recv()
        l_sib(k).start()
    sum_a(2)
    sum_g(2)
    for k in range(4):
        l_in(l_role(k) + 1 - 2 * core).wait_recv()
    for k in (1, 3, 2):
        for s in range(CAP):
            place = tables[k][s]
            pack[k, s] = loc[lax.rem(place[0], 8), place[1]]
        slots(k).start()
    for s in range(CAP):
        place = tables[0][s]
        got[zh, s] = loc[lax.rem(place[0], 8), place[1]]

    eye = jnp.where(lax.broadcasted_iota(jnp.int32, (BLK, BLK), 0) == lax.broadcasted_iota(jnp.int32, (BLK, BLK), 1),
                    jnp.float32(damping), jnp.float32(0.0))

    def block_at(n, i, j, width=BLK):
        b = mat[n, i * BLK:(i + 1) * BLK, j * BLK:j * BLK + width] * scale
        if i == j:
            diag = b[:, 0:BLK] + eye
            b = diag if width == BLK else jnp.concatenate([diag, b[:, BLK:]], 1)
        return b

    for n in range(2):
        for i in range(4):
            mat[n, i * BLK:(i + 1) * BLK, i * BLK:PANEL] = block_at(n, i, i, PANEL - i * BLK)

    x = mat[:, 0:BLK, 0:BLK]
    for kk in range(4):
        lo, hi = kk * BLK, (kk + 1) * BLK
        factor_blocks(x, inv0.at[kk])
        sum_w(kk)
        li = [inv0[kk, n] for n in range(2)]
        if kk < 3:
            first = [dot32(li[n], mat[n, lo:hi, hi:hi + BLK], ((1,), (0,))) for n in range(2)]
            first_t = [v.T for v in first]
            x = jnp.stack([
                mat[n, hi:hi + BLK, hi:hi + BLK] - dot32(first_t[n], first[n], ((1,), (0,))) for n in range(2)])
        for n in range(2):
            mat[n, lo:hi, PANEL + lo:PANEL + hi] = li[n]
            if kk < 3:
                rest = PANEL + lo - hi - BLK
                if rest:
                    mat[n, lo:hi, hi + BLK:PANEL + lo] = dot32(li[n], mat[n, lo:hi, hi + BLK:PANEL + lo], ((1,), (0,)))
                row = mat[n, lo:hi, hi + BLK:PANEL + hi]
                mat[n, hi:hi + BLK, hi + BLK:PANEL + hi] = mat[n, hi:hi + BLK, hi + BLK:PANEL + hi] - dot32(
                    first_t[n], row, ((1,), (0,)))
                for i in range(kk + 2, 4):
                    ut = mat[n, lo:hi, i * BLK:(i + 1) * BLK].T
                    mat[n, i * BLK:(i + 1) * BLK, i * BLK:PANEL + hi] = mat[
                        n, i * BLK:(i + 1) * BLK, i * BLK:PANEL + hi] - dot32(
                        ut, mat[n, lo:hi, i * BLK:PANEL + hi], ((1,), (0,)))
            elif kk == 3:
                mat[n, lo:hi, PANEL:PANEL + lo] = dot32(li[n], mat[n, lo:hi, PANEL:PANEL + lo], ((1,), (0,)))
            invt[n, 0:hi, lo:hi] = mat[n, lo:hi, PANEL:PANEL + hi].T

    mine = pl.multiple_of(f * 16, 16)
    picked[8 * CAP:, :] = dot32(mat[1, pl.ds(mine, 16), PANEL:] * scale, wmat[...], ((1,), (0,)))
    for k in range(1, 4):
        src = lax.rem(zh + k, 4)
        copy(pack.at[k], got.at[src], s_g.at[k], r_g.at[src], (d, z_peer(k))).wait_recv()
    table = tables[0]
    for s in range(CAP):
        picked[8 * s:8 * s + 8, :] = got[lax.div(table[s][0], 8), s]
    def times_inverse(n, rows):
        left = dot32(rows[:, 0:256], invt[n, 0:256, 0:256], ((1,), (0,)))
        return jnp.concatenate([left, dot32(rows, invt[n, :, 256:PANEL], ((1,), (0,)))], 1)

    ra = times_inverse(0, picked[...])
    rg = times_inverse(1, picked[0:8 * CAP, :])
    pre_out[...] = ra[8 * CAP:, :]
    for s in range(CAP):
        lo, hi = 8 * s, 8 * s + 8
        out = jnp.where(jnp.full((8, PANEL), table[s][2]) == 1, ra[lo:hi, :], rg[lo:hi, :])
        rows_out[s] = jnp.where(jnp.full((8, PANEL), table[s][3]) == 1, out, 0.0)

    @pl.when(f == 0)
    def _():
        give_g.wait_send()

    @pl.when(f == 1)
    def _():
        give_z1.wait_send()

    @pl.when(f == 2)
    def _():
        give_t3.wait_send()

    @pl.when(f < 2)
    def _():
        for k in (1, 2, 3):
            own_x(k).wait_send()

    @pl.when(zh == 0)
    def _():
        for k in (1, 2, 3):
            own_z(k).wait_send()

    for way in range(2):
        own_to_x(way, lambda c: c.wait_send())
    for k in range(1, 16):
        features(k).wait_send()
        for way in range(2):
            x_copy(k // 4, k % 4, way).wait_send()
    for k in range(16):
        sibling(k // 4, k % 4).wait_send()
    for k in (1, 2, 3):
        z_copy(k).wait_send()
        l_x(k).wait_send()
        slots(k).wait_send()
    for dz in range(4):
        for way in range(2):
            y_copy(dz, way).wait_send()
            far_copy(dz, way).wait_send()
        l_sib(dz).wait_send()


def window(owners, acts_t, grads_out):
    vmem = pl.BlockSpec(memory_space=pltpu.VMEM)
    dma = pltpu.SemaphoreType.DMA
    f32, bf16 = jnp.float32, jnp.bfloat16
    return pl.pallas_call(
        kernel,
        out_shape=(
            jax.ShapeDtypeStruct((CAP, 8, PANEL), f32),
            jax.ShapeDtypeStruct((16, PANEL), f32),
        ),
        in_specs=[pl.BlockSpec(memory_space=pltpu.HBM)] * 3,
        out_specs=(vmem, vmem),
        scratch_shapes=[
            pltpu.SMEM((NT,), jnp.int32),
            pltpu.VMEM((192, 128), bf16),
            pltpu.VMEM((128, 384), bf16),
            pltpu.VMEM((16, FROWS, 128), bf16),
            pltpu.VMEM((128, 256), bf16),
            pltpu.VMEM((2, 16, 128, PANEL), bf16),
            pltpu.VMEM((16, FROWS, 128), bf16),
            pltpu.VMEM((128, 256), bf16),
            pltpu.VMEM((2, PANEL, 2 * PANEL), f32),
            pltpu.VMEM((4, 2, BLK, BLK), f32),
            pltpu.VMEM((2, PANEL, PANEL), f32),
            pltpu.VMEM((PANEL, PANEL), f32),
            pltpu.VMEM((FROWS, PANEL), f32),
            pltpu.VMEM((8, GROUPS, 8, PANEL), f32),
            pltpu.VMEM((4, CAP, 8, PANEL), f32),
            pltpu.VMEM((4, CAP, 8, PANEL), f32),
            pltpu.VMEM((8 * CAP + 16, PANEL), f32),
            dma((3,)),
            dma((1,)), dma((3,)), dma((4,)), dma((4,)), dma,
            dma((4,)), dma((16,)), dma((4, 2)),
            dma((4, 2)), dma((2, 16)),
            dma((2, 16)), dma((2, 16)),
            dma((16,)), dma((16,)),
            dma((16,)), dma((16,)),
            dma((4,)), dma((4,)), dma((8,)),
            dma((4,)), dma((4,)),
        ],
        compiler_params=pltpu.CompilerParams(
            collective_id=0, has_side_effects=True, vmem_limit_bytes=60 * 2**20),
        name="window",
    )(owners, acts_t, grads_out)


def on_device(acts, grads_out, owners):
    rows, pre = window(owners, acts.T, grads_out)
    return rows[None], pre


def solution(mesh):
    return jax.shard_map(
        on_device,
        mesh=mesh,
        in_specs=(P("dp", "factor"), P("dp", "factor"), P()),
        out_specs=(P("factor", None, "dp", None), P("factor", None)),
        check_vma=False,
    )
```

```python
import jax
import jax.numpy as jnp
from jax import lax
from jax.experimental import pallas as pl
from jax.experimental.pallas import tpu as pltpu
from jax.sharding import PartitionSpec as P

D = 6144
PANEL = 512
TILE = 128
NT = 136
TILES_A = (D - PANEL) // TILE
CAP = 6
BLK = 128
GROUPS = 5
FROWS = 48

damping = 0.1
MESH = pl.DeviceIdType.MESH
HIGH = lax.Precision.HIGHEST


def lanes(x, c):
    return jnp.broadcast_to(x[:, :, c:c + 1], x.shape)


def rows8(x, j):
    return jnp.broadcast_to(x[:, j:j + 1, :], x.shape)


def recip(x):
    r = pl.reciprocal(x, approx=True)
    r = r * (2.0 - x * r)
    return r * (2.0 - x * r)


def pair(ba, bb, j):
    p00, p01, p11 = rows8(ba, j), rows8(bb, j), rows8(bb, j + 1)
    det = p00 * p11 - p01 * p01
    r0, rd = recip(p00), recip(det)
    return p00, p01, det, r0, rd


def strip16(x0, x1, w0, w1, c0, sub):
    b0 = [lanes(x0, c0 + j) for j in range(8)]
    b1 = [lanes(x1, c0 + j) for j in range(16)]
    d0 = jnp.ones(x0.shape, jnp.float32)
    d1 = d0
    for j in range(0, 8, 2):
        ba, bb = b0[j], b0[j + 1]
        p00, p01, det, r0, rd = pair(ba, bb, j)
        d0 = jnp.where(sub == j, p00, jnp.where(sub == j + 1, det * r0, d0))
        q = p01 * r0
        m0a = jnp.where(sub > j, ba, 0.0) * r0
        m0b = jnp.where(sub > j + 1, bb * p00 - ba * p01, 0.0) * rd
        m1a = b1[j] * r0
        m1b = (b1[j + 1] * p00 - b1[j] * p01) * rd
        for k in range(j + 2, 8):
            ra = rows8(b0[k], j)
            rb = rows8(b0[k], j + 1) - q * ra
            b0[k] = b0[k] - m0a * ra - m0b * rb
            b1[k] = b1[k] - m1a * ra - m1b * rb
        for k in range(8, 16):
            ra = rows8(b1[j], k - 8)
            rb = rows8(b1[j + 1], k - 8) - q * ra
            b1[k] = b1[k] - m1a * ra - m1b * rb
        ra = rows8(x0, j)
        rb = rows8(x0, j + 1) - q * ra
        x0 = x0 - m0a * ra - m0b * rb
        x1 = x1 - m1a * ra - m1b * rb
        ra = rows8(w0, j)
        rb = rows8(w0, j + 1) - q * ra
        w0 = w0 - m0a * ra - m0b * rb
        w1 = w1 - m1a * ra - m1b * rb
    for j in range(0, 8, 2):
        ba, bb = b1[8 + j], b1[9 + j]
        p00, p01, det, r0, rd = pair(ba, bb, j)
        d1 = jnp.where(sub == j, p00, jnp.where(sub == j + 1, det * r0, d1))
        q = p01 * r0
        ma = jnp.where(sub > j, ba, 0.0) * r0
        mb = jnp.where(sub > j + 1, bb * p00 - ba * p01, 0.0) * rd
        for k in range(j + 2, 8):
            ra = rows8(b1[8 + k], j)
            rb = rows8(b1[8 + k], j + 1) - q * ra
            b1[8 + k] = b1[8 + k] - ma * ra - mb * rb
        ra = rows8(x1, j)
        rb = rows8(x1, j + 1) - q * ra
        x1 = x1 - ma * ra - mb * rb
        ra = rows8(w1, j)
        rb = rows8(w1, j + 1) - q * ra
        w1 = w1 - ma * ra - mb * rb
    s0, s1 = lax.rsqrt(d0), lax.rsqrt(d1)
    s0 = s0 * (1.5 - 0.5 * d0 * s0 * s0)
    s1 = s1 * (1.5 - 0.5 * d1 * s1 * s1)
    return x0 * s0, x1 * s1, w0 * s0, w1 * s1


def factor_blocks(x, out):
    sub = lax.broadcasted_iota(jnp.int32, (2, 8, BLK), 1)
    w = jnp.where(lax.broadcasted_iota(jnp.int32, (2, BLK, BLK), 1)
                  == lax.broadcasted_iota(jnp.int32, (2, BLK, BLK), 2), 1.0, 0.0).astype(jnp.float32)
    for i in range(8):
        v0, v1, u0, u1 = strip16(x[:, 0:8], x[:, 8:16], w[:, 0:8], w[:, 8:16], 16 * i, sub)
        out[:, 16 * i:16 * i + 8, :] = u0
        out[:, 16 * i + 8:16 * i + 16, :] = u1
        if i == 7:
            break
        lo = 16 * (i + 1)
        v = jnp.concatenate([v0, v1], 1)
        u = jnp.concatenate([u0, u1], 1)
        vt = jnp.stack([v[0].T, v[1].T])
        nx, nw = x[:, 16:32], w[:, 16:32]
        for j in range(16):
            m = jnp.broadcast_to(vt[:, lo:lo + 16, j:j + 1], nx.shape)
            nx = nx - m * v[:, j:j + 1, :]
            nw = nw - m * u[:, j:j + 1, :]
        if i == 6:
            x, w = nx, nw
            continue
        vu = jnp.concatenate([v, u], 2)
        less = jnp.stack([dot32(vt[n, lo + 16:, :], vu[n], ((1,), (0,))) for n in range(2)])
        x = jnp.concatenate([nx, x[:, 32:] - less[:, :, 0:BLK]], 1)
        w = jnp.concatenate([nw, w[:, 32:] - less[:, :, BLK:]], 1)


def dot32(a, b, dims):
    return lax.dot_general(a, b, (dims, ((), ())), precision=HIGH, preferred_element_type=jnp.float32)


def dot16(a, b, dims):
    return lax.dot_general(a, b, (dims, ((), ())), preferred_element_type=jnp.float32)


def owned_tables(own_ref, d, ids):
    zero = jnp.int32(0)

    def look(t, carry):
        owner = own_ref[t]
        out = []
        for n, *slots in carry:
            hit = owner == ids[len(out)]
            slots = [jnp.where(jnp.logical_and(hit, n == s), t, slots[s]) for s in range(CAP)]
            out.append((n + hit.astype(jnp.int32),) + tuple(slots))
        return tuple(out)

    found = lax.fori_loop(0, NT, look, tuple((zero,) * (CAP + 1) for _ in ids))
    p = lax.div(d, 8)
    tables = []
    for n, *slots in found:
        table = []
        for s in range(CAP):
            t = slots[s]
            half = 2 * (t + 4) + p
            fa = lax.div(half, 3)
            slot_a = lax.div(half - 3 * fa - lax.rem(3 * fa + p, 2), 2)
            tg = jnp.maximum(t - TILES_A, 0) + 4
            fg = lax.div(tg, 3)
            slot_g = 2 + tg - 3 * fg
            act = t < TILES_A
            table.append((
                jnp.where(act, fa, fg), jnp.where(act, slot_a, slot_g),
                act.astype(jnp.int32), (s < n).astype(jnp.int32)))
        tables.append(table)
    return tables


def kernel(own_in, at_in, gr_in, rows_out, pre_out,
           own_ref, act_t, gr, fs, za, pan, feat, z1, mat, inv0, invt, wmat, raw, loc, pack, got, picked,
           s_in, s_p, r_p, s_b, s_c, r_own, s_z, r_blk, s_y, s_far, r_far, s_x, r_x, s_sib, r_sib, s_f, r_f,
           s_lx, s_ls, r_l, s_g, r_g):
    d = lax.axis_index("dp")
    f = lax.axis_index("factor")
    y, zl = lax.div(d, 4), lax.rem(d, 4)
    role, zh, core = lax.rem(f, 8), lax.div(f, 8), lax.rem(f, 2)
    xx = lax.div(role, 2)
    base = f - role
    sib = f + 1 - 2 * core
    scale = 1.0 / 2048.0

    def z_peer(k):
        return lax.rem(f + 8 * k, 32)

    def x_peer(k):
        return base + 2 * lax.rem(xx + k, 4) + core

    def copy(src, dst, send, recv, to):
        return pltpu.make_async_remote_copy(
            src_ref=src, dst_ref=dst, send_sem=send, recv_sem=recv,
            device_id=to, device_id_type=MESH)

    fetch = (
        pltpu.make_async_copy(at_in, act_t, s_in.at[0]),
        pltpu.make_async_copy(gr_in, gr, s_in.at[1]),
        pltpu.make_async_copy(own_in, own_ref, s_in.at[2]),
    )
    for c in fetch:
        c.start()

    barrier = pltpu.get_barrier_semaphore()
    for k in range(1, 16):
        pl.semaphore_signal(barrier, inc=1, device_id=(lax.rem(d + k, 16), f), device_id_type=MESH)
    for k in range(1, 4):
        pl.semaphore_signal(barrier, inc=1, device_id=(d, z_peer(k)), device_id_type=MESH)
        pl.semaphore_signal(barrier, inc=1, device_id=(d, x_peer(k)), device_id_type=MESH)
    pl.semaphore_signal(barrier, inc=1, device_id=(d, sib), device_id_type=MESH)
    for c in fetch:
        c.wait()

    odd = core == 1

    @pl.when(f < 3)
    def _():
        at32 = act_t[...].astype(jnp.float32)
        gap = jnp.zeros((64, 128), jnp.float32)
        placed = jnp.where(odd, jnp.concatenate([gap, at32], 0), jnp.concatenate([at32, gap], 0))
        za[...] = placed.T.astype(jnp.bfloat16)

    pl.semaphore_wait(barrier, 22)

    h = lax.rem(xx, 2)

    def half_of(parity):
        return pl.ds(pl.multiple_of(64 * parity, 64), 64)

    def part(way):
        return pl.ds(pl.multiple_of(64 * h + 32 * way, 32), 32)

    def other_part(way):
        return pl.ds(pl.multiple_of(64 * (1 - h) + 32 * way, 32), 32)

    give_g = copy(gr, pan.at[1, d, :, pl.ds(0, 384)], s_p.at[0], r_p.at[2], (d, f + 1))
    give_z1 = copy(za, z1, s_p.at[0], r_p.at[0], (d, lax.rem(f + 31, 32)))
    give_t3 = copy(za.at[:, pl.ds(0, 128)], pan.at[0, d, :, pl.ds(384, 128)], s_p.at[0], r_p.at[1],
                   (d, lax.rem(f + 30, 32)))

    def own_x(k):
        rows = pl.ds(64 * (k % 2), 64)
        return copy(pan.at[core, d, rows], pan.at[core, d, rows], s_b.at[k], r_own, (d, x_peer(k)))

    def own_z(k):
        ref = pan.at[core, d, half_of(h)]
        return copy(ref, ref, s_c.at[k], r_own, (d, z_peer(k)))

    @pl.when(f == 0)
    def _():
        give_g.start()
        copy(za, z1, s_p.at[0], r_p.at[0], (d, f + 1)).wait_recv()
        pan[0, d, :, 0:128] = za[:, 0:128]
        pan[0, d, :, 128:256] = za[:, 128:256] + z1[:, 0:128]
        pan[0, d, :, 256:384] = z1[:, 128:256]
        copy(za.at[:, pl.ds(0, 128)], pan.at[0, d, :, pl.ds(384, 128)], s_p.at[0], r_p.at[1], (d, f + 1)).wait_recv()

    @pl.when(f == 1)
    def _():
        give_z1.start()
        pan[1, d, :, 384:512] = gr[:, 0:128]
        copy(gr, pan.at[1, d, :, pl.ds(0, 384)], s_p.at[0], r_p.at[2], (d, f + 1)).wait_recv()

    @pl.when(f == 2)
    def _():
        give_t3.start()

    @pl.when(f < 2)
    def _():
        for k in (1, 3, 2):
            own_x(k).start()

    @pl.when(jnp.logical_and(zh == 0, xx > 0))
    def _():
        own_z(1).wait_recv()

    @pl.when(zh == 0)
    def _():
        for k in (1, 3, 2):
            own_z(k).start()

    at32 = act_t[...].astype(jnp.float32)
    gt32 = gr[...].astype(jnp.float32).T
    for t in range(16):
        p, q = t // 8, t % 8
        low = at32[8 * q:8 * q + 8]
        mid = at32[64 + 8 * q:72 + 8 * q]
        top = at32[128 + 8 * q:136 + 8 * q]
        here = odd if p else jnp.logical_not(odd)
        fs[t, 0:16, :] = jnp.concatenate(
            [jnp.where(here, low, mid), jnp.where(here, top, mid)], 0).astype(jnp.bfloat16)
        gs = [gt32[128 * i + 8 * t:128 * i + 8 * t + 8] for i in range(3)]
        fs[t, 16:48, :] = jnp.concatenate(gs + [jnp.zeros_like(gs[0])], 0).astype(jnp.bfloat16)

    def features(k):
        to = lax.rem(d + k, 16)
        return copy(fs.at[to], feat.at[d], s_f.at[k], r_f.at[k], (to, f))

    for k in range(1, 16):
        features(k).start()
    feat[d] = fs[d]
    mat[...] = jnp.zeros_like(mat)
    invt[...] = jnp.zeros_like(invt)
    wmat[...] = jnp.zeros_like(wmat)
    raw[...] = jnp.zeros_like(raw)
    tables = owned_tables(own_ref, d, [f] + [z_peer(k) for k in range(1, 4)])

    @pl.when(zh > 0)
    def _():
        own_z(1).wait_recv()

    def at(dy, dz):
        return lax.rem(y + 4 - dy, 4) * 4 + lax.rem(zl + 4 - dz, 4)

    def y_dev(dy):
        return (lax.rem(y + dy, 4) * 4 + zl, f)

    def block(which, sem, to):
        ref = pan.at[core, which, half_of(h)]
        return copy(ref, ref, sem, r_blk.at[which], to)

    def z_copy(dz):
        return block(d, s_z.at[dz], (y * 4 + lax.rem(zl + dz, 4), f))

    def y_copy(dz, way):
        return block(at(0, dz), s_y.at[dz, way], y_dev((1, 3)[way]))

    def far_copy(dz, way):
        which = at((1, 3)[way], dz)
        ref = pan.at[core, which, part(way)]
        return copy(ref, ref, s_far.at[dz, way], r_far.at[way, which], y_dev((1, 3)[way]))

    def far_in(dz, way):
        which = at(2, dz)
        ref = pan.at[core, which, part(way)]
        return copy(ref, ref, s_far.at[dz, way], r_far.at[way, which], y_dev(1))

    def x_copy(dy, dz, way):
        which = at(dy, dz)
        ref = pan.at[core, which, part(way)]
        return copy(ref, ref, s_x.at[way, dy * 4 + dz], r_x.at[way, which], (d, x_peer((1, 3)[way])))

    def x_in(dy, dz, way):
        which = at(dy, dz)
        ref = pan.at[core, which, other_part(way)]
        return copy(ref, ref, s_x.at[way, 0], r_x.at[way, which], (d, x_peer(1)))

    holder = jnp.logical_and(zh == 0, xx == 0)

    def own_to_x(way, act):
        to_holder = jnp.logical_and(zh == 0, xx == (3, 1)[way])

        @pl.when(jnp.logical_not(to_holder))
        def _():
            act(x_copy(0, 0, way))

    def sibling(dy, dz):
        which = at(dy, dz)
        return copy(pan.at[core, which], pan.at[core, which], s_sib.at[dy * 4 + dz], r_sib.at[which], (d, sib))

    def whole(dy, dz):
        if dy or dz:
            for way in range(2):
                x_in(dy, dz, way).wait_recv()
        else:
            @pl.when(jnp.logical_not(holder))
            def _():
                for way in range(2):
                    x_in(dy, dz, way).wait_recv()
        sibling(dy, dz).start()

    def from_sibling(dy, dz):
        which = at(dy, dz)
        return copy(pan.at[1 - core, which], pan.at[1 - core, which], s_sib.at[1], r_sib.at[which], (d, sib))

    for dz in (1, 3, 2):
        z_copy(dz).start()
    for way in range(2):
        y_copy(0, way).start()
    for way in range(2):
        own_to_x(way, lambda c: c.start())
    for dz in (1, 3, 2):
        block(at(0, dz), s_z.at[dz], y_dev(1)).wait_recv()
        for way in range(2):
            y_copy(dz, way).start()
        for way in range(2):
            x_copy(0, dz, way).start()

    def line(dy):
        return pl.ds(pl.multiple_of(lax.rem(y + 4 - dy, 4) * 4, 4), 4)

    def ready(dy):
        for dz in range(4):
            from_sibling(dy, dz).wait_recv()

    def add_upper(n, cols, cols_t):
        mat[n, 0:256, 0:PANEL] = mat[n, 0:256, 0:PANEL] + dot16(cols_t[0:256], cols, ((1,), (0,)))
        mat[n, 256:PANEL, 256:PANEL] = mat[n, 256:PANEL, 256:PANEL] + dot16(
            cols_t[256:PANEL], cols[:, 256:PANEL], ((1,), (0,)))

    def sum_a(dy):
        pa = pan[0, line(dy)].reshape(512, PANEL)
        pat = pa.T
        add_upper(0, pa, pat)
        wmat[...] = wmat[...] + dot16(pat, pan[1, line(dy)].reshape(512, PANEL), ((1,), (0,)))

    def sum_g(dy):
        pg = pan[1, line(dy)].reshape(512, PANEL)
        add_upper(1, pg, pg.T)

    def sum_rows(dy):
        ra = jnp.zeros((16, PANEL), jnp.float32)
        rg = jnp.zeros((32, PANEL), jnp.float32)
        for dz in range(4):
            which = at(dy, dz)
            ra = ra + dot16(feat[which, 0:16, :], pan[0, which], ((1,), (0,)))
            rg = rg + dot16(feat[which, 16:48, :], pan[1, which], ((1,), (0,)))
        raw[0:16, :] = raw[0:16, :] + ra
        raw[16:48, :] = raw[16:48, :] + rg

    def near(dz):
        for way in range(2):
            block(at((1, 3)[way], dz), s_z.at[1], y_dev(1)).wait_recv()
            far_copy(dz, way).start()
            for to in range(2):
                x_copy((1, 3)[way], dz, to).start()

    def far(dz):
        for way in range(2):
            far_in(dz, way).wait_recv()
            x_copy(2, dz, way).start()

    for dz in (0, 1, 3, 2):
        near(dz)
        whole(0, dz)
    far(0)
    ready(0)
    sum_a(0)
    far(1)
    for dz in (0, 1, 3, 2):
        whole(1, dz)
    sum_g(0)
    far(3)
    for dz in (0, 1, 3, 2):
        whole(3, dz)
    ready(1)
    sum_a(1)
    far(2)
    for k in range(1, 16):
        src = lax.rem(d + 16 - k, 16)
        copy(fs.at[d], feat.at[src], s_f.at[k], r_f.at[k], (lax.rem(d + 1, 16), f)).wait_recv()
    sum_rows(0)
    sum_g(1)
    for dz in (0, 1, 3, 2):
        whole(2, dz)
    sum_rows(1)
    ready(3)
    sum_a(3)
    sum_rows(3)
    ready(2)
    sum_rows(2)

    for s in range(GROUPS):
        loc[role, s] = raw[8 * s:8 * s + 8, :] * scale

    def l_x(k):
        return copy(loc.at[role], loc.at[role], s_lx.at[k], r_l.at[role], (d, x_peer(k)))

    def l_role(k):
        return 2 * lax.rem(xx + k, 4) + core

    def l_sib(k):
        r = l_role(k)
        return copy(loc.at[r], loc.at[r], s_ls.at[k], r_l.at[r], (d, sib))

    def l_in(r):
        return copy(loc.at[r], loc.at[r], s_ls.at[0], r_l.at[r], (d, sib))

    def slots(k):
        return copy(pack.at[k], got.at[zh], s_g.at[k], r_g.at[zh], (d, z_peer(k)))

    for k in (1, 3, 2):
        l_x(k).start()
    l_sib(0).start()

    sum_g(3)
    for k in (1, 3, 2):
        l_in(l_role(k)).wait_recv()
        l_sib(k).start()
    sum_a(2)
    sum_g(2)
    for k in range(4):
        l_in(l_role(k) + 1 - 2 * core).wait_recv()
    for k in (1, 3, 2):
        for s in range(CAP):
            place = tables[k][s]
            pack[k, s] = loc[lax.rem(place[0], 8), place[1]]
        slots(k).start()
    for s in range(CAP):
        place = tables[0][s]
        got[zh, s] = loc[lax.rem(place[0], 8), place[1]]

    eye = jnp.where(lax.broadcasted_iota(jnp.int32, (BLK, BLK), 0) == lax.broadcasted_iota(jnp.int32, (BLK, BLK), 1),
                    jnp.float32(damping), jnp.float32(0.0))

    def block_at(n, i, j, width=BLK):
        b = mat[n, i * BLK:(i + 1) * BLK, j * BLK:j * BLK + width] * scale
        if i == j:
            diag = b[:, 0:BLK] + eye
            b = diag if width == BLK else jnp.concatenate([diag, b[:, BLK:]], 1)
        return b

    for n in range(2):
        for i in range(4):
            mat[n, i * BLK:(i + 1) * BLK, i * BLK:PANEL] = block_at(n, i, i, PANEL - i * BLK)

    x = mat[:, 0:BLK, 0:BLK]
    for kk in range(4):
        lo, hi = kk * BLK, (kk + 1) * BLK
        factor_blocks(x, inv0.at[kk])
        li = [inv0[kk, n] for n in range(2)]
        if kk < 3:
            first = [dot32(li[n], mat[n, lo:hi, hi:hi + BLK], ((1,), (0,))) for n in range(2)]
            first_t = [v.T for v in first]
            x = jnp.stack([
                mat[n, hi:hi + BLK, hi:hi + BLK] - dot32(first_t[n], first[n], ((1,), (0,))) for n in range(2)])
        for n in range(2):
            mat[n, lo:hi, PANEL + lo:PANEL + hi] = li[n]
            if kk < 3:
                rest = PANEL + lo - hi - BLK
                if rest:
                    mat[n, lo:hi, hi + BLK:PANEL + lo] = dot32(li[n], mat[n, lo:hi, hi + BLK:PANEL + lo], ((1,), (0,)))
                row = mat[n, lo:hi, hi + BLK:PANEL + hi]
                mat[n, hi:hi + BLK, hi + BLK:PANEL + hi] = mat[n, hi:hi + BLK, hi + BLK:PANEL + hi] - dot32(
                    first_t[n], row, ((1,), (0,)))
                for i in range(kk + 2, 4):
                    ut = mat[n, lo:hi, i * BLK:(i + 1) * BLK].T
                    mat[n, i * BLK:(i + 1) * BLK, i * BLK:PANEL + hi] = mat[
                        n, i * BLK:(i + 1) * BLK, i * BLK:PANEL + hi] - dot32(
                        ut, mat[n, lo:hi, i * BLK:PANEL + hi], ((1,), (0,)))
            elif kk == 3:
                mat[n, lo:hi, PANEL:PANEL + lo] = dot32(li[n], mat[n, lo:hi, PANEL:PANEL + lo], ((1,), (0,)))
            invt[n, 0:hi, lo:hi] = mat[n, lo:hi, PANEL:PANEL + hi].T

    mine = pl.multiple_of(f * 16, 16)
    mine_t = (mat[1, pl.ds(mine, 16), PANEL:] * scale).T
    picked[8 * CAP:, :] = dot32(wmat[...], mine_t, ((1,), (0,))).T
    for k in range(1, 4):
        src = lax.rem(zh + k, 4)
        copy(pack.at[k], got.at[src], s_g.at[k], r_g.at[src], (d, z_peer(k))).wait_recv()
    table = tables[0]
    for s in range(CAP):
        picked[8 * s:8 * s + 8, :] = got[lax.div(table[s][0], 8), s]
    def times_inverse(n, rows):
        left = dot32(rows[:, 0:256], invt[n, 0:256, 0:256], ((1,), (0,)))
        return jnp.concatenate([left, dot32(rows, invt[n, :, 256:PANEL], ((1,), (0,)))], 1)

    ra = times_inverse(0, picked[...])
    rg = times_inverse(1, picked[0:8 * CAP, :])
    pre_out[...] = ra[8 * CAP:, :]
    for s in range(CAP):
        lo, hi = 8 * s, 8 * s + 8
        out = jnp.where(jnp.full((8, PANEL), table[s][2]) == 1, ra[lo:hi, :], rg[lo:hi, :])
        rows_out[s] = jnp.where(jnp.full((8, PANEL), table[s][3]) == 1, out, 0.0)

    @pl.when(f == 0)
    def _():
        give_g.wait_send()

    @pl.when(f == 1)
    def _():
        give_z1.wait_send()

    @pl.when(f == 2)
    def _():
        give_t3.wait_send()

    @pl.when(f < 2)
    def _():
        for k in (1, 2, 3):
            own_x(k).wait_send()

    @pl.when(zh == 0)
    def _():
        for k in (1, 2, 3):
            own_z(k).wait_send()

    for way in range(2):
        own_to_x(way, lambda c: c.wait_send())
    for k in range(1, 16):
        features(k).wait_send()
        for way in range(2):
            x_copy(k // 4, k % 4, way).wait_send()
    for k in range(16):
        sibling(k // 4, k % 4).wait_send()
    for k in (1, 2, 3):
        z_copy(k).wait_send()
        l_x(k).wait_send()
        slots(k).wait_send()
    for dz in range(4):
        for way in range(2):
            y_copy(dz, way).wait_send()
            far_copy(dz, way).wait_send()
        l_sib(dz).wait_send()


def window(owners, acts_t, grads_out):
    vmem = pl.BlockSpec(memory_space=pltpu.VMEM)
    dma = pltpu.SemaphoreType.DMA
    f32, bf16 = jnp.float32, jnp.bfloat16
    return pl.pallas_call(
        kernel,
        out_shape=(
            jax.ShapeDtypeStruct((CAP, 8, PANEL), f32),
            jax.ShapeDtypeStruct((16, PANEL), f32),
        ),
        in_specs=[pl.BlockSpec(memory_space=pltpu.HBM)] * 3,
        out_specs=(vmem, vmem),
        scratch_shapes=[
            pltpu.SMEM((NT,), jnp.int32),
            pltpu.VMEM((192, 128), bf16),
            pltpu.VMEM((128, 384), bf16),
            pltpu.VMEM((16, FROWS, 128), bf16),
            pltpu.VMEM((128, 256), bf16),
            pltpu.VMEM((2, 16, 128, PANEL), bf16),
            pltpu.VMEM((16, FROWS, 128), bf16),
            pltpu.VMEM((128, 256), bf16),
            pltpu.VMEM((2, PANEL, 2 * PANEL), f32),
            pltpu.VMEM((4, 2, BLK, BLK), f32),
            pltpu.VMEM((2, PANEL, PANEL), f32),
            pltpu.VMEM((PANEL, PANEL), f32),
            pltpu.VMEM((FROWS, PANEL), f32),
            pltpu.VMEM((8, GROUPS, 8, PANEL), f32),
            pltpu.VMEM((4, CAP, 8, PANEL), f32),
            pltpu.VMEM((4, CAP, 8, PANEL), f32),
            pltpu.VMEM((8 * CAP + 16, PANEL), f32),
            dma((3,)),
            dma((1,)), dma((3,)), dma((4,)), dma((4,)), dma,
            dma((4,)), dma((16,)), dma((4, 2)),
            dma((4, 2)), dma((2, 16)),
            dma((2, 16)), dma((2, 16)),
            dma((16,)), dma((16,)),
            dma((16,)), dma((16,)),
            dma((4,)), dma((4,)), dma((8,)),
            dma((4,)), dma((4,)),
        ],
        compiler_params=pltpu.CompilerParams(
            collective_id=0, has_side_effects=True, vmem_limit_bytes=60 * 2**20),
        name="window",
    )(owners, acts_t, grads_out)


def on_device(acts, grads_out, owners):
    rows, pre = window(owners, acts.T, grads_out)
    return rows[None], pre


def solution(mesh):
    return jax.shard_map(
        on_device,
        mesh=mesh,
        in_specs=(P("dp", "factor"), P("dp", "factor"), P()),
        out_specs=(P("factor", None, "dp", None), P("factor", None)),
        check_vma=False,
    )
```
